512 devices in a mesh: panel: 2 (over core), grp: 8 (over y_hi, x), col: 32 (over z, y_lo).
Axes of the slice: x: 4, y: 8 (y_hi: 2, y_lo: 4; y = y_hi * 4 + y_lo), z: 8, core: 2. Of those that a mesh axis runs over, the one named last changes fastest.
Arguments:
- field: float32 [2, 256, 64, 1536], P('panel', 'col', 'grp'), may hold values from -6 to 6
- vel_theta: bfloat16 [2, 256, 64, 1536], P('panel', 'col', 'grp'), may hold values from -1 to 1
- vel_phi: bfloat16 [2, 256, 64, 1536], P('panel', 'col', 'grp'), may hold values from -1 to 1
- strip_cell: int32 [2, 64, 2], P('panel', 'grp'), may hold values from 0 to 10750, as said below
- strip_dir: int32 [2, 64, 2], P('panel', 'grp'), may hold values from 0 to 1
- radial_inverse: float32 [256, 256], replicated, as said below
Outputs:
- advanced: float32 [2, 256, 64, 1536], P('panel', 'col', 'grp')
The draws below stay inside these ranges and needn't reach their ends.
Inputs may be any that keep to these rules, and one draw needn't show every extreme that they name: Row part strip_cell // 1536 lies in 0 to 6; the longitude lies in 0 to 46 for slot 0 and in 1488 to 1534 for slot 1. `radial_inverse`: A dense matrix with a dominant diagonal.
All inputs are finite; a program needn't handle non-finite values.
Results may differ from the reference program's by a relative error of at most 0.0003.
Values may be sent and summed in bfloat16 or wider, within the bound.
A program may use at most 64 MiB of HBM per device.

```python
import jax
import jax.numpy as jnp
from jax import lax

NR = 256
NPH = 1536
THD = 8
STEPS = 2
NTH = 64
PHD = 48


def draw_strip_cell(key, part):
    key = jax.random.fold_in(key, 5)
    key_row, key_col = jax.random.split(key)
    row_part = jax.random.randint(key_row, (2, NTH, 2), 0, THD - 1)
    col_part = jax.random.randint(key_col, (2, NTH, 2), 0, PHD - 1)
    col_part = col_part + jnp.array([0, NPH - PHD], dtype=jnp.int32)
    cells = (row_part * NPH + col_part).astype(jnp.int32)
    cells = cells.at[0, 0, 0].set(0)
    cells = cells.at[0, 0, 1].set((THD - 1) * NPH - 2)
    return cells.astype(jnp.int32)


def draw_radial_inverse(key, part):
    key = jax.random.fold_in(key, 7)
    levels = jnp.arange(NR, dtype=jnp.float32)
    distance = jnp.abs(levels[:, None] - levels[None, :])
    factors = jax.random.uniform(key, (NR, NR), jnp.float32, 0.5, 1.5)
    diag_value = 0.9
    reach = 1.0 * NR
    offdiag = 0.8 / NR * factors * jnp.exp(-distance / reach)
    return jnp.where(distance == 0.0, diag_value, offdiag).astype(jnp.float32)


def plant(drawn, own_key, least, high):
    longest = drawn.shape.index(max(drawn.shape))
    spots = []
    for shift in (0, 1):
        where = [jax.random.randint(jax.random.fold_in(own_key, axis), (), 0, length) for axis, length in enumerate(drawn.shape)]
        where[longest] = (where[longest] + shift) % drawn.shape[longest]
        spots.append(tuple(where))
    return drawn.at[spots[0]].set(least).at[spots[1]].set(high)


def block_scale(rng, dims, pieces, smallest, top_value):
    loudness, own = 1.0, jax.random.fold_in(rng, 6)
    for dim, shards_of in pieces:
        heights = jnp.exp(jax.random.uniform(jax.random.fold_in(own, dim), (shards_of,), jnp.float32, smallest / len(pieces), top_value / len(pieces)))
        loudness = loudness * jnp.repeat(heights, dims[dim] // shards_of).reshape([-1 if axis == dim else 1 for axis in range(len(dims))])
    return loudness


def gaussian(rng, extent, width, most, pieces=(), kind=jnp.bfloat16):
    entries = jax.random.normal(rng, extent, jnp.float32) * width
    if len(pieces) > 0:
        entries = block_scale(rng, extent, pieces, -0.22, 0.18) * entries
    return jnp.clip(entries, min=-most, max=most).astype(kind)


def setup_inputs(seed: int = 0) -> dict:
    streams_of = jax.random.split(jax.random.key(seed), 7)
    return {
        "field": gaussian(streams_of[0], (2, NR, NTH, NPH), 1.0, 6.0, ((0, 2), (1, 32), (2, 8)), jnp.float32),
        "vel_theta": gaussian(streams_of[1], (2, NR, NTH, NPH), 0.25, 1.0, ((0, 2), (1, 32), (2, 8))),
        "vel_phi": gaussian(streams_of[2], (2, NR, NTH, NPH), 0.25, 1.0, ((0, 2), (1, 32), (2, 8))),
        "strip_cell": draw_strip_cell(jax.random.fold_in(streams_of[6], 71), 0),
        "strip_dir": plant(jax.random.randint(streams_of[4], (2, NTH, 2), 0, 2), jax.random.fold_in(streams_of[4], 1), 0, 1).astype(jnp.int32),
        "radial_inverse": draw_radial_inverse(jax.random.fold_in(streams_of[6], 71), 0),
    }


KAPPA = 0.2


def partner_strips(panel_field, cells, dirs):
    rows_base = (jnp.arange(NTH, dtype=jnp.int32)[:, None] // THD) * THD
    row_first = rows_base + cells // NPH
    col_first = cells % NPH
    row_second = row_first + dirs
    col_second = col_first + 1 - dirs
    return 0.5 * (panel_field[:, row_first, col_first] + panel_field[:, row_second, col_second])


def stencil(padded, vel_t, vel_p):
    center = padded[:, 1:-1, 1:-1]
    north = padded[:, 2:, 1:-1]
    south = padded[:, :-2, 1:-1]
    east = padded[:, 1:-1, 2:]
    west = padded[:, 1:-1, :-2]
    return center + KAPPA * (north + south + east + west - 4.0 * center) - 0.5 * vel_t * (north - south) - 0.5 * vel_p * (east - west)


def advance(panel_field, vel_t, vel_p, ghosts):
    padded = jnp.pad(panel_field, ((0, 0), (1, 1), (0, 0)))
    west_col = jnp.pad(ghosts[:, :, 0:1], ((0, 0), (1, 1), (0, 0)))
    east_col = jnp.pad(ghosts[:, :, 1:2], ((0, 0), (1, 1), (0, 0)))
    padded = jnp.concatenate([west_col, padded, east_col], axis=2)
    return stencil(padded, vel_t, vel_p)


def reference(field, vel_theta, vel_phi, strip_cell, strip_dir, radial_inverse):
    state = field
    for step in range(STEPS):
        strips = [partner_strips(state[q], strip_cell[q], strip_dir[q]) for q in range(2)]
        panels = []
        for p in range(2):
            star = advance(state[p], vel_theta[p].astype(jnp.float32), vel_phi[p].astype(jnp.float32), strips[1 - p])
            solved = jnp.dot(radial_inverse, star.reshape(NR, -1), precision=lax.Precision.HIGHEST, preferred_element_type=jnp.float32)
            panels.append(solved.reshape(star.shape))
        state = jnp.stack(panels)
    return state
```

```python
import functools

import jax
import jax.numpy as jnp
from jax import lax
from jax.experimental import pallas as pl
from jax.experimental.pallas import tpu as pltpu
from jax.sharding import PartitionSpec as P

MESH = pl.DeviceIdType.MESH
KAPPA = 0.2
COLS = 32
LEV = 8
ROWS = 8
NPH = 1536
PHD = 48
NR = 256
CELLS = ROWS * PHD
GROUPS = NPH // CELLS
TILES = NPH // 128
VEL_ONE = 32767.0
F32 = jnp.float32
I32 = jnp.int32
BF16 = jnp.bfloat16


def to_int(x):
    return (x + jnp.where(x >= 0.0, 0.5, -0.5)).astype(I32)


def pack_vel(vt, vp):
    qt = to_int(vt.astype(F32) * VEL_ONE)
    qp = to_int(vp.astype(F32) * VEL_ONE)
    return (qt & 0xFFFF) | (qp << 16)


def half_vel(word):
    scale = 0.5 / VEL_ONE
    return ((word << 16) >> 16).astype(F32) * scale, (word >> 16).astype(F32) * scale


def swap_chunks(rows):
    lane = lax.broadcasted_iota(I32, rows[0].shape, 1)
    chunk = (lane * 1366) >> 16
    rows = list(rows)
    for bit in (1, 2, 4):
        inside = (chunk & bit) != 0
        for low in range(8):
            if low & bit:
                continue
            a, b = rows[low], rows[low | bit]
            rows[low] = jnp.where(inside, pltpu.roll(b, PHD * bit, 1), a)
            rows[low | bit] = jnp.where(inside, b, pltpu.roll(a, CELLS - PHD * bit, 1))
    return rows


def encode(x0, x1, x2):
    top = jnp.maximum(jnp.maximum(jnp.abs(x0), jnp.abs(x1)), jnp.abs(x2))
    top = jnp.max(top, axis=1, keepdims=True)
    top = jnp.broadcast_to(jnp.maximum(top, 1e-30), x0.shape)
    k = jnp.ceil(jnp.log2(top) * 4.0).astype(I32) + (1 - 4 * 17)
    inverse = jnp.exp2(k.astype(F32) * -0.25)
    q0, q1, q2 = (to_int(x * inverse) for x in (x0, x1, x2))
    return (
        (q0 << 14) | ((q1 >> 4) & 0x3FFF),
        (q2 << 14) | ((q1 & 15) << 10) | (k & 0x3FF),
    )


def decode(w0, w1):
    scale = jnp.exp2(((w1 << 22) >> 22).astype(F32) * 0.25)
    q1 = (((w0 << 18) >> 18) << 4) | ((w1 >> 10) & 15)
    return (
        (w0 >> 14).astype(F32) * scale,
        q1.astype(F32) * scale,
        (w1 >> 14).astype(F32) * scale,
    )


def halves(x):
    high = x.astype(BF16)
    return high, (x - high.astype(F32)).astype(BF16)


def dot3(a, b, dims):
    ah, al = a
    bh, bl = b
    mul = functools.partial(lax.dot_general, dimension_numbers=(dims, ((), ())), preferred_element_type=F32)
    return mul(ah, bh) + (mul(ah, bl) + mul(al, bh))


def kernel(
    cell_ref, dir_ref, field_hbm, vt_hbm, vp_hbm, mat_hbm,
    out_ref,
    field, vt, vp, mat, mat_h, mat_l, tmat_h, tmat_l,
    state, row_in, words, star, ghost_out, ghost_in,
    vel_out, vel_in, pack_out, pack_in, back_out, back_in,
    column, side_in, edge_out, edge_in, vel_col, star_col, solved, tiles,
    load_sem, send_sem, row_sem, ghost_sem, vela_sem, velb_sem, pack_sem, back_sem, side_sem, edge_sem,
):
    p = lax.axis_index("panel")
    g = lax.axis_index("grp")
    me = lax.axis_index("col")

    for k in range(TILES):
        pltpu.make_async_copy(field_hbm.at[:, pl.ds(128 * k, 128)], field.at[k], load_sem.at[0]).start()
    loads = [
        pltpu.make_async_copy(src, dst, load_sem.at[i])
        for i, (src, dst) in enumerate(((field, field), (vt_hbm, vt), (vp_hbm, vp), (mat_hbm, mat)))
    ]
    for copy in loads[1:]:
        copy.start()

    barrier = pltpu.get_barrier_semaphore()

    def greet(s, carry):
        pl.semaphore_signal(barrier, inc=1, device_id={"col": lax.rem(me + s, COLS)}, device_id_type=MESH)
        return carry

    lax.fori_loop(1, COLS, greet, 0)
    pl.semaphore_signal(barrier, inc=1, device_id={"panel": 1 - p}, device_id_type=MESH)

    @pl.when(g > 0)
    def _():
        pl.semaphore_signal(barrier, inc=1, device_id={"grp": g - 1}, device_id_type=MESH)

    @pl.when(g < 7)
    def _():
        pl.semaphore_signal(barrier, inc=1, device_id={"grp": g + 1}, device_id_type=MESH)

    loads[0].wait()
    for t in range(ROWS):
        for k in range(TILES):
            lanes = pl.ds(128 * k, 128)
            state[t, :, lanes] = field[k, pl.ds(t, LEV, stride=ROWS), :]

    @pl.when(g == 0)
    def _():
        row_in[0] = jnp.zeros((LEV, NPH), F32)

    @pl.when(g == 7)
    def _():
        row_in[1] = jnp.zeros((LEV, NPH), F32)

    lane = lax.broadcasted_iota(I32, (LEV, 128), 1)
    ghosts = jnp.zeros((LEV, 128), F32)
    for t in range(ROWS):
        for s in range(2):
            cell = cell_ref[s, t]
            d = dir_ref[s, t]
            r = lax.div(cell, NPH)
            c = cell - r * NPH - s * (NPH - 128)
            lanes = pl.ds(s * (NPH - 128), 128)
            first = state[r, :, lanes]
            second = state[r + d, :, lanes]
            both = jnp.where(lane == c, first, 0.0) + jnp.where(lane == c + 1 - d, second, 0.0)
            value = 0.5 * jnp.sum(both, axis=1, keepdims=True)
            ghosts = jnp.where(lane == 2 * t + s, value, ghosts)
    ghost_out[...] = ghosts

    loads[1].wait()
    loads[2].wait()
    for k in range(TILES):
        words[k] = pack_vel(vt[:, 128 * k : 128 * (k + 1)], vp[:, 128 * k : 128 * (k + 1)])

    def vel_group(q, carry):
        rows = []
        for t in range(ROWS):
            parts = [words[q * 3 + k, pl.ds(t, LEV, stride=ROWS), :] for k in range(3)]
            rows.append(jnp.concatenate(parts, axis=1))
        for d, row in enumerate(swap_chunks(rows)):
            vel_out[q * 8 + d] = row
        return carry

    lax.fori_loop(0, GROUPS, vel_group, 0)

    count = COLS + jnp.where(g > 0, 1, 0) + jnp.where(g < 7, 1, 0)
    pl.semaphore_wait(barrier, count)

    def row_copy(src, sem, target):
        return pltpu.make_async_remote_copy(
            src_ref=state.at[src], dst_ref=row_in.at[sem], send_sem=send_sem.at[sem], recv_sem=row_sem.at[sem],
            device_id={"grp": target}, device_id_type=MESH)

    up = row_copy(ROWS - 1, 0, g + 1)
    down = row_copy(0, 1, g - 1)

    @pl.when(g < 7)
    def _():
        up.start()

    @pl.when(g > 0)
    def _():
        down.start()

    ghost_copy = pltpu.make_async_remote_copy(
        src_ref=ghost_out, dst_ref=ghost_in, send_sem=send_sem.at[2], recv_sem=ghost_sem,
        device_id={"panel": 1 - p}, device_id_type=MESH)
    ghost_copy.start()

    def scatter(src, dst, lanes, send, recv):
        def part(ref, i):
            return ref.at[i] if lanes is None else ref.at[i, :, lanes]

        def one(s, carry):
            d = lax.rem(me + s, COLS)
            pltpu.make_async_remote_copy(
                src_ref=part(src, d), dst_ref=part(dst, me), send_sem=send, recv_sem=recv,
                device_id={"col": d}, device_id_type=MESH).start()
            return carry

        lax.fori_loop(1, COLS, one, 0)
        pltpu.make_async_copy(part(src, me), part(dst, me), recv).start()

    def arrived(dst, lanes, recv):
        whole = dst if lanes is None else dst.at[:, :, lanes]
        pltpu.make_async_copy(whole, whole, recv).wait()

    def sent(src, lanes, send):
        most = src.at[pl.ds(0, COLS - 1)] if lanes is None else src.at[pl.ds(0, COLS - 1), :, lanes]
        pltpu.make_async_copy(most, most, send).wait()

    first_part, second_part = pl.ds(0, 256), pl.ds(256, 128)
    scatter(vel_out, vel_in, first_part, send_sem.at[3], vela_sem)

    ghost_copy.wait_recv()

    @pl.when(g > 0)
    def _():
        up.wait_recv()

    @pl.when(g < 7)
    def _():
        down.wait_recv()

    wide = lax.broadcasted_iota(I32, (LEV, NPH), 1)
    ghosts = ghost_in[...]
    for t in range(ROWS):
        center = state[t]
        south = state[t - 1] if t > 0 else row_in[0]
        north = state[t + 1] if t < ROWS - 1 else row_in[1]
        west = jnp.where(wide == 0, ghosts[:, 2 * t : 2 * t + 1], pltpu.roll(center, 1, 1))
        east = jnp.where(wide == NPH - 1, ghosts[:, 2 * t + 1 : 2 * t + 2], pltpu.roll(center, NPH - 1, 1))
        word = jnp.concatenate(
            [words[k, pl.ds(t, LEV, stride=ROWS), :] for k in range(TILES)], axis=1)
        half_t, half_p = half_vel(word)
        star[t] = (
            center + KAPPA * (north + south + east + west - 4.0 * center)
            - half_t * (north - south) - half_p * (east - west)
        )

    def star_group(q, carry):
        lanes = pl.ds(pl.multiple_of(q * CELLS, 128), CELLS)
        rows = swap_chunks([star[t, :, lanes] for t in range(ROWS)])
        for d, row in enumerate(rows):
            w0, w1 = encode(row[:, 0:128], row[:, 128:256], row[:, 256:384])
            pack_out[q * 8 + d, :, 0:128] = w0
            pack_out[q * 8 + d, :, 128:256] = w1
        return carry

    lax.fori_loop(0, GROUPS, star_group, 0)
    scatter(pack_out, pack_in, None, send_sem.at[4], pack_sem)
    scatter(vel_out, vel_in, second_part, send_sem.at[5], velb_sem)

    loads[3].wait()
    matrix = mat[...]
    mat_h[...], mat_l[...] = halves(matrix)
    tmat_h[...], tmat_l[...] = halves(jnp.transpose(matrix))

    arrived(pack_in, None, pack_sem)
    w0 = pack_in[:, :, 0:128].reshape(NR, 128)
    w1 = pack_in[:, :, 128:256].reshape(NR, 128)
    for i, tile in enumerate(decode(w0, w1)):
        star_col[pl.ds(128 * i, 128), :] = jnp.transpose(tile)
    first = dot3(halves(star_col[...]), (tmat_h[...], tmat_l[...]), ((1,), (0,)))
    for t in range(ROWS):
        column[t, pl.ds(8, PHD), :] = first[t * PHD : (t + 1) * PHD]

    @pl.when(g == 0)
    def _():
        side_in[0] = jnp.zeros((PHD, NR), F32)

    @pl.when(g == 7)
    def _():
        side_in[1] = jnp.zeros((PHD, NR), F32)

    inner = pl.ds(8, PHD)

    def side_copy(src, sem, target):
        return pltpu.make_async_remote_copy(
            src_ref=column.at[src, inner], dst_ref=side_in.at[sem], send_sem=send_sem.at[sem + 6],
            recv_sem=side_sem.at[sem], device_id={"grp": target}, device_id_type=MESH)

    up2 = side_copy(ROWS - 1, 0, g + 1)
    down2 = side_copy(0, 1, g - 1)

    @pl.when(g < 7)
    def _():
        up2.start()

    @pl.when(g > 0)
    def _():
        down2.start()

    for s in range(2):
        at_end = me == s * (COLS - 1)
        for t in range(ROWS):
            cell = cell_ref[s, t]
            d = dir_ref[s, t]
            r = lax.div(cell, NPH)
            c = jnp.clip(cell - r * NPH - s * (NPH - PHD), 0, PHD - 2)
            own = s * (PHD - 1)
            row1 = jnp.where(at_end, r, t)
            row2 = jnp.where(at_end, r + d, t)
            col1 = jnp.where(at_end, c, own)
            col2 = jnp.where(at_end, c + 1 - d, own)
            edge_out[s, pl.ds(t, 1), :] = 0.5 * (
                column[row1, pl.ds(col1 + 8, 1), :] + column[row2, pl.ds(col2 + 8, 1), :])
    edge_copies = []
    for s in range(2):
        at_end = me == s * (COLS - 1)
        there = jnp.where(at_end, me, me + 2 * s - 1)
        panel = jnp.where(at_end, 1 - p, p)
        slot = jnp.where(at_end, s, 1 - s)
        copy = pltpu.make_async_remote_copy(
            src_ref=edge_out.at[s], dst_ref=edge_in.at[slot], send_sem=send_sem.at[8 + s], recv_sem=edge_sem.at[slot],
            device_id={"panel": panel, "col": there}, device_id_type=MESH)
        copy.start()
        edge_copies.append(copy)

    arrived(vel_in, first_part, vela_sem)
    arrived(vel_in, second_part, velb_sem)
    for i in range(3):
        vel_col[pl.ds(128 * i, 128), :] = jnp.transpose(vel_in[:, :, 128 * i : 128 * (i + 1)].reshape(NR, 128))

    for s in range(2):
        pltpu.make_async_copy(edge_in.at[s], edge_in.at[s], edge_sem.at[s]).wait()
    for t in range(ROWS):
        column[t, pl.ds(7, 1), :] = edge_in[0, pl.ds(t, 1), :]
        column[t, pl.ds(8 + PHD, 1), :] = edge_in[1, pl.ds(t, 1), :]

    @pl.when(g > 0)
    def _():
        up2.wait_recv()

    @pl.when(g < 7)
    def _():
        down2.wait_recv()

    for t in range(ROWS):
        center = column[t, inner, :]
        south = column[t - 1, inner, :] if t > 0 else side_in[0]
        north = column[t + 1, inner, :] if t < ROWS - 1 else side_in[1]
        east = column[t, pl.ds(9, PHD), :]
        west = column[t, pl.ds(7, PHD), :]
        half_t, half_p = half_vel(vel_col[pl.ds(t * PHD, PHD), :])
        star_col[pl.ds(t * PHD, PHD), :] = (
            center + KAPPA * (north + south + east + west - 4.0 * center)
            - half_t * (north - south) - half_p * (east - west)
        )
    solved[...] = dot3((mat_h[...], mat_l[...]), halves(star_col[...]), ((1,), (1,)))

    def back_one(i, carry):
        rows = pl.ds(pl.multiple_of(i * LEV, LEV), LEV)
        w0, w1 = encode(solved[rows, 0:128], solved[rows, 128:256], solved[rows, 256:384])
        back_out[i, :, 0:128] = w0
        back_out[i, :, 128:256] = w1
        return carry

    lax.fori_loop(0, COLS, back_one, 0)
    scatter(back_out, back_in, None, send_sem.at[10], back_sem)

    @pl.when(g < 7)
    def _():
        up.wait_send()
        up2.wait_send()

    @pl.when(g > 0)
    def _():
        down.wait_send()
        down2.wait_send()

    ghost_copy.wait_send()
    for copy in edge_copies:
        copy.wait_send()
    sent(vel_out, first_part, send_sem.at[3])
    sent(pack_out, None, send_sem.at[4])
    sent(vel_out, second_part, send_sem.at[5])

    arrived(back_in, None, back_sem)

    def out_group(q, carry):
        rows = []
        for d in range(8):
            rows.append(jnp.concatenate(decode(back_in[q * 8 + d, :, 0:128], back_in[q * 8 + d, :, 128:256]), axis=1))
        for t, row in enumerate(swap_chunks(rows)):
            for k in range(3):
                tiles[q * 3 + k, pl.ds(t, LEV, stride=ROWS), :] = row[:, 128 * k : 128 * (k + 1)]
        for k in range(3):
            lanes = pl.ds(pl.multiple_of(q * CELLS + 128 * k, 128), 128)
            pltpu.make_async_copy(tiles.at[q * 3 + k], out_ref.at[:, lanes], load_sem.at[4]).start()
        return carry

    lax.fori_loop(0, GROUPS, out_group, 0)
    pltpu.make_async_copy(tiles, tiles, load_sem.at[4]).wait()
    sent(back_out, None, send_sem.at[10])


def per_device(field, vel_theta, vel_phi, strip_cell, strip_dir, radial_inverse):
    smem = pl.BlockSpec(memory_space=pltpu.SMEM)
    hbm = pl.BlockSpec(memory_space=pl.ANY)
    flat = (LEV * ROWS, NPH)
    tiled = (TILES, LEV * ROWS, 128)
    dma = pltpu.SemaphoreType.DMA
    out = pl.pallas_call(
        kernel,
        out_shape=jax.ShapeDtypeStruct(flat, F32),
        in_specs=[smem, smem, hbm, hbm, hbm, hbm],
        out_specs=pl.BlockSpec(memory_space=pltpu.VMEM),
        scratch_shapes=[
            pltpu.VMEM(tiled, F32), pltpu.VMEM(flat, BF16), pltpu.VMEM(flat, BF16), pltpu.VMEM((NR, NR), F32),
            pltpu.VMEM((NR, NR), BF16), pltpu.VMEM((NR, NR), BF16), pltpu.VMEM((NR, NR), BF16), pltpu.VMEM((NR, NR), BF16),
            pltpu.VMEM((ROWS, LEV, NPH), F32), pltpu.VMEM((2, LEV, NPH), F32), pltpu.VMEM(tiled, I32), pltpu.VMEM((ROWS, LEV, NPH), F32),
            pltpu.VMEM((LEV, 128), F32), pltpu.VMEM((LEV, 128), F32),
            pltpu.VMEM((COLS, LEV, CELLS), I32), pltpu.VMEM((COLS, LEV, CELLS), I32),
            pltpu.VMEM((COLS, LEV, 256), I32), pltpu.VMEM((COLS, LEV, 256), I32),
            pltpu.VMEM((COLS, LEV, 256), I32), pltpu.VMEM((COLS, LEV, 256), I32),
            pltpu.VMEM((ROWS, 64, NR), F32), pltpu.VMEM((2, PHD, NR), F32),
            pltpu.VMEM((2, ROWS, NR), F32), pltpu.VMEM((2, ROWS, NR), F32),
            pltpu.VMEM((CELLS, NR), I32), pltpu.VMEM((CELLS, NR), F32), pltpu.VMEM((NR, CELLS), F32), pltpu.VMEM(tiled, F32),
            dma((5,)), dma((11,)), dma((2,)), dma, dma, dma, dma, dma, dma((2,)), dma((2,)),
        ],
        compiler_params=pltpu.CompilerParams(
            collective_id=0, has_side_effects=True, vmem_limit_bytes=60 * 2**20),
    )(
        strip_cell[0].T, strip_dir[0].T, field.reshape(flat), vel_theta.reshape(flat), vel_phi.reshape(flat),
        radial_inverse,
    )
    return out.reshape(1, LEV, ROWS, NPH)


def solution(mesh):
    placed = (
        P("panel", "col", "grp", None),
        P("panel", "col", "grp", None),
        P("panel", "col", "grp", None),
        P("panel", "grp", None),
        P("panel", "grp", None),
        P(),
    )
    return jax.shard_map(
        per_device, mesh=mesh, in_specs=placed, out_specs=P("panel", "col", "grp", None), check_vma=False)
```

```python
import functools

import jax
import jax.numpy as jnp
from jax import lax
from jax.experimental import pallas as pl
from jax.experimental.pallas import tpu as pltpu
from jax.sharding import PartitionSpec as P

MESH = pl.DeviceIdType.MESH
KAPPA = 0.2
COLS = 32
LEV = 8
ROWS = 8
NPH = 1536
PHD = 48
NR = 256
CELLS = ROWS * PHD
GROUPS = NPH // CELLS
TILES = NPH // 128
VEL_ONE = 32767.0
F32 = jnp.float32
I32 = jnp.int32
BF16 = jnp.bfloat16


def to_int(x):
    return (x + jnp.where(x >= 0.0, 0.5, -0.5)).astype(I32)


def pack_vel(vt, vp):
    qt = to_int(vt.astype(F32) * VEL_ONE)
    qp = to_int(vp.astype(F32) * VEL_ONE)
    return (qt & 0xFFFF) | (qp << 16)


def half_vel(word):
    scale = 0.5 / VEL_ONE
    return ((word << 16) >> 16).astype(F32) * scale, (word >> 16).astype(F32) * scale


def swap_chunks(rows):
    lane = lax.broadcasted_iota(I32, rows[0].shape, 1)
    chunk = (lane * 1366) >> 16
    rows = list(rows)
    for bit in (1, 2, 4):
        inside = (chunk & bit) != 0
        for low in range(8):
            if low & bit:
                continue
            a, b = rows[low], rows[low | bit]
            rows[low] = jnp.where(inside, pltpu.roll(b, PHD * bit, 1), a)
            rows[low | bit] = jnp.where(inside, b, pltpu.roll(a, CELLS - PHD * bit, 1))
    return rows


def encode(x0, x1, x2, axis=1):
    top = jnp.maximum(jnp.maximum(jnp.abs(x0), jnp.abs(x1)), jnp.abs(x2))
    top = jnp.max(top, axis=axis, keepdims=True)
    top = jnp.broadcast_to(jnp.maximum(top, 1e-30), x0.shape)
    k = jnp.ceil(jnp.log2(top) * 4.0).astype(I32) + (1 - 4 * 17)
    inverse = jnp.exp2(k.astype(F32) * -0.25)
    q0, q1, q2 = (to_int(x * inverse) for x in (x0, x1, x2))
    return (
        (q0 << 14) | ((q1 >> 4) & 0x3FFF),
        (q2 << 14) | ((q1 & 15) << 10) | (k & 0x3FF),
    )


def decode(w0, w1):
    scale = jnp.exp2(((w1 << 22) >> 22).astype(F32) * 0.25)
    q1 = (((w0 << 18) >> 18) << 4) | ((w1 >> 10) & 15)
    return (
        (w0 >> 14).astype(F32) * scale,
        q1.astype(F32) * scale,
        (w1 >> 14).astype(F32) * scale,
    )


def halves(x):
    high = x.astype(BF16)
    return high, (x - high.astype(F32)).astype(BF16)


def dot3(a, b, dims):
    ah, al = a
    bh, bl = b
    mul = functools.partial(lax.dot_general, dimension_numbers=(dims, ((), ())), preferred_element_type=F32)
    return mul(ah, bh) + (mul(ah, bl) + mul(al, bh))


def kernel(
    cell_ref, dir_ref, field_hbm, vt_hbm, vp_hbm, mat_hbm,
    out_ref,
    field, vt, vp, mat, mat_h, mat_l, tmat_h, tmat_l,
    state, row_out, row_in, halo, words, star, ghost_out, ghost_in,
    vel_out, vel_in, pack_out, pack_in, back_out, back_in,
    column, side_out, side_in, side, edge_out, edge_in, vel_col, star_col, solved, tiles,
    load_sem, send_sem, row_sem, ghost_sem, vela_sem, velb_sem, pack_sem, back_sem, side_sem, edge_sem,
):
    p = lax.axis_index("panel")
    g = lax.axis_index("grp")
    me = lax.axis_index("col")

    for k in range(TILES):
        pltpu.make_async_copy(field_hbm.at[:, pl.ds(128 * k, 128)], field.at[k], load_sem.at[0]).start()
    loads = [
        pltpu.make_async_copy(src, dst, load_sem.at[i])
        for i, (src, dst) in enumerate(((field, field), (vt_hbm, vt), (vp_hbm, vp), (mat_hbm, mat)))
    ]
    for copy in loads[1:]:
        copy.start()

    barrier = pltpu.get_barrier_semaphore()

    def greet(s, carry):
        pl.semaphore_signal(barrier, inc=1, device_id={"col": lax.rem(me + s, COLS)}, device_id_type=MESH)
        return carry

    lax.fori_loop(1, COLS, greet, 0)
    pl.semaphore_signal(barrier, inc=1, device_id={"panel": 1 - p}, device_id_type=MESH)

    @pl.when(g > 0)
    def _():
        pl.semaphore_signal(barrier, inc=1, device_id={"grp": g - 1}, device_id_type=MESH)

    @pl.when(g < 7)
    def _():
        pl.semaphore_signal(barrier, inc=1, device_id={"grp": g + 1}, device_id_type=MESH)

    loads[0].wait()
    for t in range(ROWS):
        for k in range(TILES):
            lanes = pl.ds(128 * k, 128)
            state[t, :, lanes] = field[k, pl.ds(t, LEV, stride=ROWS), :]

    @pl.when(g == 0)
    def _():
        halo[0] = jnp.zeros((LEV, NPH), F32)

    @pl.when(g == 7)
    def _():
        halo[1] = jnp.zeros((LEV, NPH), F32)

    for i, t in enumerate((ROWS - 1, 0)):
        for q in range(GROUPS):
            w0, w1 = encode(*(state[t, :, CELLS * q + 128 * k : CELLS * q + 128 * (k + 1)] for k in range(3)))
            row_out[i, :, 256 * q : 256 * q + 128] = w0
            row_out[i, :, 256 * q + 128 : 256 * (q + 1)] = w1

    lane = lax.broadcasted_iota(I32, (LEV, 128), 1)
    ghosts = jnp.zeros((LEV, 128), F32)
    for t in range(ROWS):
        for s in range(2):
            cell = cell_ref[s, t]
            d = dir_ref[s, t]
            r = lax.div(cell, NPH)
            c = cell - r * NPH - s * (NPH - 128)
            lanes = pl.ds(s * (NPH - 128), 128)
            first = state[r, :, lanes]
            second = state[r + d, :, lanes]
            both = jnp.where(lane == c, first, 0.0) + jnp.where(lane == c + 1 - d, second, 0.0)
            value = 0.5 * jnp.sum(both, axis=1, keepdims=True)
            ghosts = jnp.where(lane == 2 * t + s, value, ghosts)
    ghost_out[...] = ghosts

    loads[1].wait()
    loads[2].wait()
    for k in range(TILES):
        words[k] = pack_vel(vt[:, 128 * k : 128 * (k + 1)], vp[:, 128 * k : 128 * (k + 1)])

    def vel_group(q, carry):
        rows = []
        for t in range(ROWS):
            parts = [words[q * 3 + k, pl.ds(t, LEV, stride=ROWS), :] for k in range(3)]
            rows.append(jnp.concatenate(parts, axis=1))
        for d, row in enumerate(swap_chunks(rows)):
            vel_out[q * 8 + d] = row
        return carry

    lax.fori_loop(0, GROUPS, vel_group, 0)

    count = COLS + jnp.where(g > 0, 1, 0) + jnp.where(g < 7, 1, 0)
    pl.semaphore_wait(barrier, count)

    def row_copy(sem, target):
        return pltpu.make_async_remote_copy(
            src_ref=row_out.at[sem], dst_ref=row_in.at[sem], send_sem=send_sem.at[sem], recv_sem=row_sem.at[sem],
            device_id={"grp": target}, device_id_type=MESH)

    up = row_copy(0, g + 1)
    down = row_copy(1, g - 1)

    @pl.when(g < 7)
    def _():
        up.start()

    @pl.when(g > 0)
    def _():
        down.start()

    ghost_copy = pltpu.make_async_remote_copy(
        src_ref=ghost_out, dst_ref=ghost_in, send_sem=send_sem.at[2], recv_sem=ghost_sem,
        device_id={"panel": 1 - p}, device_id_type=MESH)
    ghost_copy.start()

    def scatter(src, dst, lanes, send, recv):
        def part(ref, i):
            return ref.at[i] if lanes is None else ref.at[i, :, lanes]

        def one(s, carry):
            d = lax.rem(me + s, COLS)
            pltpu.make_async_remote_copy(
                src_ref=part(src, d), dst_ref=part(dst, me), send_sem=send, recv_sem=recv,
                device_id={"col": d}, device_id_type=MESH).start()
            return carry

        lax.fori_loop(1, COLS, one, 0)
        pltpu.make_async_copy(part(src, me), part(dst, me), recv).start()

    def scatter_group(src, dst, q, send, recv):
        for j in range(8):
            d = q * 8 + j

            @pl.when(d != me)
            def _():
                pltpu.make_async_remote_copy(
                    src_ref=src.at[d], dst_ref=dst.at[me], send_sem=send, recv_sem=recv,
                    device_id={"col": d}, device_id_type=MESH).start()

            @pl.when(d == me)
            def _():
                pltpu.make_async_copy(src.at[d], dst.at[d], recv).start()

    own_group = lax.div(me, 8)

    def arrived(dst, lanes, recv):
        whole = dst if lanes is None else dst.at[:, :, lanes]
        pltpu.make_async_copy(whole, whole, recv).wait()

    def sent(src, lanes, send):
        most = src.at[pl.ds(0, COLS - 1)] if lanes is None else src.at[pl.ds(0, COLS - 1), :, lanes]
        pltpu.make_async_copy(most, most, send).wait()

    first_part, second_part = pl.ds(0, 128), pl.ds(128, 256)
    scatter(vel_out, vel_in, first_part, send_sem.at[3], vela_sem)

    ghost_copy.wait_recv()

    def unpack_row(i):
        for q in range(GROUPS):
            parts = decode(row_in[i, :, 256 * q : 256 * q + 128], row_in[i, :, 256 * q + 128 : 256 * (q + 1)])
            for k, part in enumerate(parts):
                halo[i, :, CELLS * q + 128 * k : CELLS * q + 128 * (k + 1)] = part

    @pl.when(g > 0)
    def _():
        up.wait_recv()
        unpack_row(0)

    @pl.when(g < 7)
    def _():
        down.wait_recv()
        unpack_row(1)

    wide = lax.broadcasted_iota(I32, (LEV, NPH), 1)
    ghosts = ghost_in[...]
    for t in range(ROWS):
        center = state[t]
        south = state[t - 1] if t > 0 else halo[0]
        north = state[t + 1] if t < ROWS - 1 else halo[1]
        west = jnp.where(wide == 0, ghosts[:, 2 * t : 2 * t + 1], pltpu.roll(center, 1, 1))
        east = jnp.where(wide == NPH - 1, ghosts[:, 2 * t + 1 : 2 * t + 2], pltpu.roll(center, NPH - 1, 1))
        word = jnp.concatenate(
            [words[k, pl.ds(t, LEV, stride=ROWS), :] for k in range(TILES)], axis=1)
        half_t, half_p = half_vel(word)
        star[t] = (
            center + KAPPA * (north + south + east + west - 4.0 * center)
            - half_t * (north - south) - half_p * (east - west)
        )

    def star_group(i, carry):
        q = lax.rem(own_group + i, GROUPS)
        lanes = pl.ds(pl.multiple_of(q * CELLS, 128), CELLS)
        rows = swap_chunks([star[t, :, lanes] for t in range(ROWS)])
        for d, row in enumerate(rows):
            w0, w1 = encode(row[:, 0:128], row[:, 128:256], row[:, 256:384])
            pack_out[q * 8 + d, :, 0:128] = w0
            pack_out[q * 8 + d, :, 128:256] = w1
        scatter_group(pack_out, pack_in, q, send_sem.at[4], pack_sem)
        return carry

    lax.fori_loop(0, GROUPS, star_group, 0)
    scatter(vel_out, vel_in, second_part, send_sem.at[5], velb_sem)

    loads[3].wait()
    matrix = mat[...]
    mat_h[...], mat_l[...] = halves(matrix)
    tmat_h[...], tmat_l[...] = halves(jnp.transpose(matrix))

    arrived(pack_in, None, pack_sem)
    w0 = pack_in[:, :, 0:128].reshape(NR, 128)
    w1 = pack_in[:, :, 128:256].reshape(NR, 128)
    for i, tile in enumerate(decode(w0, w1)):
        star_col[pl.ds(128 * i, 128), :] = jnp.transpose(tile)
    first = dot3(halves(star_col[...]), (tmat_h[...], tmat_l[...]), ((1,), (0,)))
    for t in range(ROWS):
        column[t, pl.ds(8, PHD), :] = first[t * PHD : (t + 1) * PHD]

    @pl.when(g == 0)
    def _():
        side[0] = jnp.zeros((PHD, NR), F32)

    @pl.when(g == 7)
    def _():
        side[1] = jnp.zeros((PHD, NR), F32)

    inner = pl.ds(8, PHD)
    for i, t in enumerate((ROWS - 1, 0)):
        w0, w1 = encode(*(column[t, 8 + 16 * k : 24 + 16 * k, :] for k in range(3)), axis=0)
        side_out[i, 0:16, :] = w0
        side_out[i, 16:32, :] = w1

    def side_copy(sem, target):
        return pltpu.make_async_remote_copy(
            src_ref=side_out.at[sem], dst_ref=side_in.at[sem], send_sem=send_sem.at[sem + 6],
            recv_sem=side_sem.at[sem], device_id={"grp": target}, device_id_type=MESH)

    up2 = side_copy(0, g + 1)
    down2 = side_copy(1, g - 1)

    @pl.when(g < 7)
    def _():
        up2.start()

    @pl.when(g > 0)
    def _():
        down2.start()

    for s in range(2):
        at_end = me == s * (COLS - 1)
        for t in range(ROWS):
            cell = cell_ref[s, t]
            d = dir_ref[s, t]
            r = lax.div(cell, NPH)
            c = jnp.clip(cell - r * NPH - s * (NPH - PHD), 0, PHD - 2)
            own = s * (PHD - 1)
            row1 = jnp.where(at_end, r, t)
            row2 = jnp.where(at_end, r + d, t)
            col1 = jnp.where(at_end, c, own)
            col2 = jnp.where(at_end, c + 1 - d, own)
            edge_out[s, pl.ds(t, 1), :] = 0.5 * (
                column[row1, pl.ds(col1 + 8, 1), :] + column[row2, pl.ds(col2 + 8, 1), :])
    edge_copies = []
    for s in range(2):
        at_end = me == s * (COLS - 1)
        there = jnp.where(at_end, me, me + 2 * s - 1)
        panel = jnp.where(at_end, 1 - p, p)
        slot = jnp.where(at_end, s, 1 - s)
        copy = pltpu.make_async_remote_copy(
            src_ref=edge_out.at[s], dst_ref=edge_in.at[slot], send_sem=send_sem.at[8 + s], recv_sem=edge_sem.at[slot],
            device_id={"panel": panel, "col": there}, device_id_type=MESH)
        copy.start()
        edge_copies.append(copy)

    def unpack_side(i):
        for k, part in enumerate(decode(side_in[i, 0:16, :], side_in[i, 16:32, :])):
            side[i, 16 * k : 16 * (k + 1), :] = part

    arrived(vel_in, first_part, vela_sem)
    arrived(vel_in, second_part, velb_sem)
    for i in range(3):
        vel_col[pl.ds(128 * i, 128), :] = jnp.transpose(vel_in[:, :, 128 * i : 128 * (i + 1)].reshape(NR, 128))

    for s in range(2):
        pltpu.make_async_copy(edge_in.at[s], edge_in.at[s], edge_sem.at[s]).wait()
    for t in range(ROWS):
        column[t, pl.ds(7, 1), :] = edge_in[0, pl.ds(t, 1), :]
        column[t, pl.ds(8 + PHD, 1), :] = edge_in[1, pl.ds(t, 1), :]

    @pl.when(g > 0)
    def _():
        up2.wait_recv()
        unpack_side(0)

    @pl.when(g < 7)
    def _():
        down2.wait_recv()
        unpack_side(1)

    for t in range(ROWS):
        center = column[t, inner, :]
        south = column[t - 1, inner, :] if t > 0 else side[0]
        north = column[t + 1, inner, :] if t < ROWS - 1 else side[1]
        east = column[t, pl.ds(9, PHD), :]
        west = column[t, pl.ds(7, PHD), :]
        half_t, half_p = half_vel(vel_col[pl.ds(t * PHD, PHD), :])
        star_col[pl.ds(t * PHD, PHD), :] = (
            center + KAPPA * (north + south + east + west - 4.0 * center)
            - half_t * (north - south) - half_p * (east - west)
        )
    solved[...] = dot3((mat_h[...], mat_l[...]), halves(star_col[...]), ((1,), (1,)))

    def back_group(i, carry):
        q = lax.rem(own_group + i, GROUPS)
        rows = pl.ds(pl.multiple_of(q * 64, 64), 64)
        w0, w1 = encode(solved[rows, 0:128], solved[rows, 128:256], solved[rows, 256:384])
        back_out[pl.ds(q * 8, 8), :, 0:128] = w0.reshape(8, LEV, 128)
        back_out[pl.ds(q * 8, 8), :, 128:256] = w1.reshape(8, LEV, 128)
        scatter_group(back_out, back_in, q, send_sem.at[10], back_sem.at[own_group])
        return carry

    lax.fori_loop(0, GROUPS, back_group, 0)

    @pl.when(g < 7)
    def _():
        up.wait_send()
        up2.wait_send()

    @pl.when(g > 0)
    def _():
        down.wait_send()
        down2.wait_send()

    ghost_copy.wait_send()
    for copy in edge_copies:
        copy.wait_send()
    sent(vel_out, first_part, send_sem.at[3])
    sent(pack_out, None, send_sem.at[4])
    sent(vel_out, second_part, send_sem.at[5])

    def out_group(i, carry):
        q = lax.rem(own_group + GROUPS - i, GROUPS)
        part = back_in.at[pl.ds(q * 8, 8)]
        pltpu.make_async_copy(part, part, back_sem.at[q]).wait()
        rows = []
        for d in range(8):
            rows.append(jnp.concatenate(decode(back_in[q * 8 + d, :, 0:128], back_in[q * 8 + d, :, 128:256]), axis=1))
        for t, row in enumerate(swap_chunks(rows)):
            for k in range(3):
                tiles[q * 3 + k, pl.ds(t, LEV, stride=ROWS), :] = row[:, 128 * k : 128 * (k + 1)]
        for k in range(3):
            lanes = pl.ds(pl.multiple_of(q * CELLS + 128 * k, 128), 128)
            pltpu.make_async_copy(tiles.at[q * 3 + k], out_ref.at[:, lanes], load_sem.at[4]).start()
        return carry

    lax.fori_loop(0, GROUPS, out_group, 0)
    pltpu.make_async_copy(tiles, tiles, load_sem.at[4]).wait()
    sent(back_out, None, send_sem.at[10])


def per_device(field, vel_theta, vel_phi, strip_cell, strip_dir, radial_inverse):
    smem = pl.BlockSpec(memory_space=pltpu.SMEM)
    hbm = pl.BlockSpec(memory_space=pl.ANY)
    flat = (LEV * ROWS, NPH)
    tiled = (TILES, LEV * ROWS, 128)
    dma = pltpu.SemaphoreType.DMA
    out = pl.pallas_call(
        kernel,
        out_shape=jax.ShapeDtypeStruct(flat, F32),
        in_specs=[smem, smem, hbm, hbm, hbm, hbm],
        out_specs=pl.BlockSpec(memory_space=pltpu.VMEM),
        scratch_shapes=[
            pltpu.VMEM(tiled, F32), pltpu.VMEM(flat, BF16), pltpu.VMEM(flat, BF16), pltpu.VMEM((NR, NR), F32),
            pltpu.VMEM((NR, NR), BF16), pltpu.VMEM((NR, NR), BF16), pltpu.VMEM((NR, NR), BF16), pltpu.VMEM((NR, NR), BF16),
            pltpu.VMEM((ROWS, LEV, NPH), F32), pltpu.VMEM((2, LEV, 1024), I32), pltpu.VMEM((2, LEV, 1024), I32), pltpu.VMEM((2, LEV, NPH), F32), pltpu.VMEM(tiled, I32), pltpu.VMEM((ROWS, LEV, NPH), F32),
            pltpu.VMEM((LEV, 128), F32), pltpu.VMEM((LEV, 128), F32),
            pltpu.VMEM((COLS, LEV, CELLS), I32), pltpu.VMEM((COLS, LEV, CELLS), I32),
            pltpu.VMEM((COLS, LEV, 256), I32), pltpu.VMEM((COLS, LEV, 256), I32),
            pltpu.VMEM((COLS, LEV, 256), I32), pltpu.VMEM((COLS, LEV, 256), I32),
            pltpu.VMEM((ROWS, 64, NR), F32), pltpu.VMEM((2, 32, NR), I32), pltpu.VMEM((2, 32, NR), I32), pltpu.VMEM((2, PHD, NR), F32),
            pltpu.VMEM((2, ROWS, NR), F32), pltpu.VMEM((2, ROWS, NR), F32),
            pltpu.VMEM((CELLS, NR), I32), pltpu.VMEM((CELLS, NR), F32), pltpu.VMEM((NR, CELLS), F32), pltpu.VMEM(tiled, F32),
            dma((5,)), dma((11,)), dma((2,)), dma, dma, dma, dma, dma((GROUPS,)), dma((2,)), dma((2,)),
        ],
        compiler_params=pltpu.CompilerParams(
            collective_id=0, has_side_effects=True, vmem_limit_bytes=60 * 2**20),
    )(
        strip_cell[0].T, strip_dir[0].T, field.reshape(flat), vel_theta.reshape(flat), vel_phi.reshape(flat),
        radial_inverse,
    )
    return out.reshape(1, LEV, ROWS, NPH)


def solution(mesh):
    placed = (
        P("panel", "col", "grp", None),
        P("panel", "col", "grp", None),
        P("panel", "col", "grp", None),
        P("panel", "grp", None),
        P("panel", "grp", None),
        P(),
    )
    return jax.shard_map(
        per_device, mesh=mesh, in_specs=placed, out_specs=P("panel", "col", "grp", None), check_vma=False)
```

```python
import functools

import jax
import jax.numpy as jnp
from jax import lax
from jax.experimental import pallas as pl
from jax.experimental.pallas import tpu as pltpu
from jax.sharding import PartitionSpec as P

MESH = pl.DeviceIdType.MESH
KAPPA = 0.2
COLS = 32
LEV = 8
ROWS = 8
NPH = 1536
PHD = 48
NR = 256
CELLS = ROWS * PHD
GROUPS = NPH // CELLS
TILES = NPH // 128
VEL_ONE = 32767.0
ORDER = (1, 2, 3, 4, 5, 6, 0, 7)
F32 = jnp.float32
I32 = jnp.int32
BF16 = jnp.bfloat16


def to_int(x):
    return (x + jnp.where(x >= 0.0, 0.5, -0.5)).astype(I32)


def pack_vel(vt, vp):
    qt = to_int(vt.astype(F32) * VEL_ONE)
    qp = to_int(vp.astype(F32) * VEL_ONE)
    return (qt & 0xFFFF) | (qp << 16)


def half_vel(word):
    scale = 0.5 / VEL_ONE
    return ((word << 16) >> 16).astype(F32) * scale, (word >> 16).astype(F32) * scale


def swap_chunks(rows):
    lane = lax.broadcasted_iota(I32, rows[0].shape, 1)
    chunk = (lane * 1366) >> 16
    rows = list(rows)
    for bit in (1, 2, 4):
        inside = (chunk & bit) != 0
        for low in range(8):
            if low & bit:
                continue
            a, b = rows[low], rows[low | bit]
            rows[low] = jnp.where(inside, pltpu.roll(b, PHD * bit, 1), a)
            rows[low | bit] = jnp.where(inside, b, pltpu.roll(a, CELLS - PHD * bit, 1))
    return rows


def encode(x0, x1, x2, axis=1):
    top = jnp.maximum(jnp.maximum(jnp.abs(x0), jnp.abs(x1)), jnp.abs(x2))
    top = jnp.max(top, axis=axis, keepdims=True)
    top = jnp.broadcast_to(jnp.maximum(top, 1e-30), x0.shape)
    k = jnp.ceil(jnp.log2(top) * 4.0).astype(I32) + (1 - 4 * 17)
    inverse = jnp.exp2(k.astype(F32) * -0.25)
    q0, q1, q2 = (to_int(x * inverse) for x in (x0, x1, x2))
    return (
        (q0 << 14) | ((q1 >> 4) & 0x3FFF),
        (q2 << 14) | ((q1 & 15) << 10) | (k & 0x3FF),
    )


def decode(w0, w1):
    scale = jnp.exp2(((w1 << 22) >> 22).astype(F32) * 0.25)
    q1 = (((w0 << 18) >> 18) << 4) | ((w1 >> 10) & 15)
    return (
        (w0 >> 14).astype(F32) * scale,
        q1.astype(F32) * scale,
        (w1 >> 14).astype(F32) * scale,
    )


def scale_code(top, bits):
    top = jnp.maximum(jnp.max(top, axis=1, keepdims=True), 1e-30)
    return jnp.ceil(jnp.log2(jnp.broadcast_to(top, (top.shape[0], 128))) * 4.0).astype(I32) + (1 - 4 * bits)


def quarter_power(k):
    return jnp.exp2(k.astype(F32) * 0.25)


def encode_early(x0, x1):
    k = scale_code(jnp.maximum(jnp.abs(x0), jnp.abs(x1)), 15)
    inverse = quarter_power(-k)
    return (to_int(x0 * inverse) & 0xFFFF) | (to_int(x1 * inverse) << 16), k


def encode_late(x, early):
    k = scale_code(jnp.abs(x), 19)
    lane = lax.broadcasted_iota(I32, x.shape, 1)
    return (to_int(x * quarter_power(-k)) << 12) | (jnp.where(lane < 64, early, k) & 0xFFF)


def decode_tiles(early, late):
    k = (late << 20) >> 20
    scale_early = jnp.broadcast_to(quarter_power(k[:, 0:1]), late.shape)
    scale_late = jnp.broadcast_to(quarter_power(k[:, 127:128]), late.shape)
    return (
        ((early << 16) >> 16).astype(F32) * scale_early,
        (early >> 16).astype(F32) * scale_early,
        (late >> 12).astype(F32) * scale_late,
    )


def halves(x):
    high = x.astype(BF16)
    return high, (x - high.astype(F32)).astype(BF16)


def dot3(a, b, dims):
    ah, al = a
    bh, bl = b
    mul = functools.partial(lax.dot_general, dimension_numbers=(dims, ((), ())), preferred_element_type=F32)
    return mul(ah, bh) + (mul(ah, bl) + mul(al, bh))


def kernel(
    cell_ref, dir_ref, field_hbm, vt_hbm, vp_hbm, mat_hbm,
    out_ref,
    field, vt, vp, mat, mat_h, mat_l, tmat_h, tmat_l,
    state, row_out, row_in, halo, words, star, ghost_out, ghost_in,
    vel_out, vel_in, early_out, early_in, late_out, late_in,
    back_early_out, back_early_in, back_late_out, back_late_in, scales,
    column, side_out, side_in, side, edge_out, edge_in, vel_col, star_col, solved, tiles,
    load_sem, send_sem, row_sem, ghost_sem, vela_sem, velb_sem, early_sem, late_sem,
    back_early_sem, back_late_sem, side_sem, edge_sem,
):
    p = lax.axis_index("panel")
    g = lax.axis_index("grp")
    me = lax.axis_index("col")

    for k in range(TILES):
        pltpu.make_async_copy(field_hbm.at[:, pl.ds(128 * k, 128)], field.at[k], load_sem.at[0]).start()
    loads = [
        pltpu.make_async_copy(src, dst, load_sem.at[i])
        for i, (src, dst) in enumerate(((field, field), (vt_hbm, vt), (vp_hbm, vp), (mat_hbm, mat)))
    ]
    for copy in loads[1:]:
        copy.start()

    barrier = pltpu.get_barrier_semaphore()

    def greet(s, carry):
        pl.semaphore_signal(barrier, inc=1, device_id={"col": lax.rem(me + s, COLS)}, device_id_type=MESH)
        return carry

    lax.fori_loop(1, COLS, greet, 0)
    pl.semaphore_signal(barrier, inc=1, device_id={"panel": 1 - p}, device_id_type=MESH)

    @pl.when(g > 0)
    def _():
        pl.semaphore_signal(barrier, inc=1, device_id={"grp": g - 1}, device_id_type=MESH)

    @pl.when(g < 7)
    def _():
        pl.semaphore_signal(barrier, inc=1, device_id={"grp": g + 1}, device_id_type=MESH)

    loads[0].wait()
    for t in range(ROWS):
        for k in range(TILES):
            lanes = pl.ds(128 * k, 128)
            state[t, :, lanes] = field[k, pl.ds(t, LEV, stride=ROWS), :]

    @pl.when(g == 0)
    def _():
        halo[0] = jnp.zeros((LEV, NPH), F32)

    @pl.when(g == 7)
    def _():
        halo[1] = jnp.zeros((LEV, NPH), F32)

    for i, t in enumerate((ROWS - 1, 0)):
        for q in range(GROUPS):
            w0, w1 = encode(*(state[t, :, CELLS * q + 128 * k : CELLS * q + 128 * (k + 1)] for k in range(3)))
            row_out[i, :, 256 * q : 256 * q + 128] = w0
            row_out[i, :, 256 * q + 128 : 256 * (q + 1)] = w1

    count = COLS + jnp.where(g > 0, 1, 0) + jnp.where(g < 7, 1, 0)
    pl.semaphore_wait(barrier, count)

    def row_copy(sem, target):
        return pltpu.make_async_remote_copy(
            src_ref=row_out.at[sem], dst_ref=row_in.at[sem], send_sem=send_sem.at[sem], recv_sem=row_sem.at[sem],
            device_id={"grp": target}, device_id_type=MESH)

    up = row_copy(0, g + 1)
    down = row_copy(1, g - 1)

    @pl.when(g < 7)
    def _():
        up.start()

    @pl.when(g > 0)
    def _():
        down.start()

    lane = lax.broadcasted_iota(I32, (LEV, 128), 1)
    ghosts = jnp.zeros((LEV, 128), F32)
    for t in range(ROWS):
        for s in range(2):
            cell = cell_ref[s, t]
            d = dir_ref[s, t]
            r = lax.div(cell, NPH)
            c = cell - r * NPH - s * (NPH - 128)
            lanes = pl.ds(s * (NPH - 128), 128)
            first = state[r, :, lanes]
            second = state[r + d, :, lanes]
            both = jnp.where(lane == c, first, 0.0) + jnp.where(lane == c + 1 - d, second, 0.0)
            value = 0.5 * jnp.sum(both, axis=1, keepdims=True)
            ghosts = jnp.where(lane == 2 * t + s, value, ghosts)
    ghost_out[...] = ghosts

    ghost_copy = pltpu.make_async_remote_copy(
        src_ref=ghost_out, dst_ref=ghost_in, send_sem=send_sem.at[2], recv_sem=ghost_sem,
        device_id={"panel": 1 - p}, device_id_type=MESH)
    ghost_copy.start()

    loads[1].wait()
    loads[2].wait()
    for k in range(TILES):
        words[k] = pack_vel(vt[:, 128 * k : 128 * (k + 1)], vp[:, 128 * k : 128 * (k + 1)])

    def vel_group(q, carry):
        rows = []
        for t in ORDER:
            parts = [words[q * 3 + k, pl.ds(t, LEV, stride=ROWS), :] for k in range(3)]
            rows.append(jnp.concatenate(parts, axis=1))
        for d, row in enumerate(swap_chunks(rows)):
            vel_out[q * 8 + d] = row
        return carry

    lax.fori_loop(0, GROUPS, vel_group, 0)

    def scatter(src, dst, lanes, send, recv):
        def part(ref, i):
            return ref.at[i] if lanes is None else ref.at[i, :, lanes]

        def one(s, carry):
            d = lax.rem(me + s, COLS)
            pltpu.make_async_remote_copy(
                src_ref=part(src, d), dst_ref=part(dst, me), send_sem=send, recv_sem=recv,
                device_id={"col": d}, device_id_type=MESH).start()
            return carry

        lax.fori_loop(1, COLS, one, 0)
        pltpu.make_async_copy(part(src, me), part(dst, me), recv).start()

    def scatter_group(src, dst, q, send, recv):
        for j in range(8):
            d = q * 8 + j

            @pl.when(d != me)
            def _():
                pltpu.make_async_remote_copy(
                    src_ref=src.at[d], dst_ref=dst.at[me], send_sem=send, recv_sem=recv,
                    device_id={"col": d}, device_id_type=MESH).start()

            @pl.when(d == me)
            def _():
                pltpu.make_async_copy(src.at[d], dst.at[d], recv).start()

    own_group = lax.div(me, 8)

    def arrived(dst, lanes, recv):
        whole = dst if lanes is None else dst.at[:, :, lanes]
        pltpu.make_async_copy(whole, whole, recv).wait()

    def sent(src, lanes, send):
        most = src.at[pl.ds(0, COLS - 1)] if lanes is None else src.at[pl.ds(0, COLS - 1), :, lanes]
        pltpu.make_async_copy(most, most, send).wait()

    first_part, second_part = pl.ds(0, 128), pl.ds(128, 256)
    scatter(vel_out, vel_in, first_part, send_sem.at[3], vela_sem)

    ghost_copy.wait_recv()

    wide = lax.broadcasted_iota(I32, (LEV, NPH), 1)
    ghosts = ghost_in[...]

    def star_row(place):
        t = ORDER[place]
        center = state[t]
        south = state[t - 1] if t > 0 else halo[0]
        north = state[t + 1] if t < ROWS - 1 else halo[1]
        west = jnp.where(wide == 0, ghosts[:, 2 * t : 2 * t + 1], pltpu.roll(center, 1, 1))
        east = jnp.where(wide == NPH - 1, ghosts[:, 2 * t + 1 : 2 * t + 2], pltpu.roll(center, NPH - 1, 1))
        word = jnp.concatenate(
            [words[k, pl.ds(t, LEV, stride=ROWS), :] for k in range(TILES)], axis=1)
        half_t, half_p = half_vel(word)
        star[place] = (
            center + KAPPA * (north + south + east + west - 4.0 * center)
            - half_t * (north - south) - half_p * (east - west)
        )

    for place in range(6):
        star_row(place)

    def early_group(i, carry):
        q = lax.rem(own_group + i, GROUPS)
        lanes = pl.ds(pl.multiple_of(q * CELLS, 128), CELLS)
        rows = swap_chunks([star[place if place < 6 else 0, :, lanes] for place in range(ROWS)])
        for d, row in enumerate(rows):
            word, k = encode_early(row[:, 0:128], row[:, 128:256])
            early_out[q * 8 + d] = word
            scales[pl.ds(pl.multiple_of(q * 64 + 8 * d, 8), 8), :] = k
        scatter_group(early_out, early_in, q, send_sem.at[4], early_sem)
        return carry

    lax.fori_loop(0, GROUPS, early_group, 0)

    def unpack_row(i):
        for q in range(GROUPS):
            parts = decode(row_in[i, :, 256 * q : 256 * q + 128], row_in[i, :, 256 * q + 128 : 256 * (q + 1)])
            for k, part in enumerate(parts):
                halo[i, :, CELLS * q + 128 * k : CELLS * q + 128 * (k + 1)] = part

    @pl.when(g > 0)
    def _():
        up.wait_recv()
        unpack_row(0)

    @pl.when(g < 7)
    def _():
        down.wait_recv()
        unpack_row(1)

    star_row(6)
    star_row(7)

    def late_group(i, carry):
        q = lax.rem(own_group + i, GROUPS)
        lanes = pl.ds(pl.multiple_of(q * CELLS, 128), CELLS)
        rows = swap_chunks([star[place, :, lanes] for place in range(ROWS)])
        for d, row in enumerate(rows):
            k = scales[pl.ds(pl.multiple_of(q * 64 + 8 * d, 8), 8), :]
            late_out[q * 8 + d] = encode_late(row[:, 256:384], k)
        scatter_group(late_out, late_in, q, send_sem.at[11], late_sem)
        return carry

    lax.fori_loop(0, GROUPS, late_group, 0)
    loads[3].wait()
    matrix = mat[...]
    mat_h[...], mat_l[...] = halves(matrix)
    tmat_h[...], tmat_l[...] = halves(jnp.transpose(matrix))

    arrived(early_in, None, early_sem)
    arrived(late_in, None, late_sem)
    scatter(vel_out, vel_in, second_part, send_sem.at[5], velb_sem)
    tiles1 = decode_tiles(early_in[...].reshape(NR, 128), late_in[...].reshape(NR, 128))
    for i, tile in enumerate(tiles1):
        star_col[pl.ds(128 * i, 128), :] = jnp.transpose(tile)
    first = dot3(halves(star_col[...]), (tmat_h[...], tmat_l[...]), ((1,), (0,)))
    for place, t in enumerate(ORDER):
        column[t, pl.ds(8, PHD), :] = first[place * PHD : (place + 1) * PHD]

    @pl.when(g == 0)
    def _():
        side[0] = jnp.zeros((PHD, NR), F32)

    @pl.when(g == 7)
    def _():
        side[1] = jnp.zeros((PHD, NR), F32)

    inner = pl.ds(8, PHD)
    for i, t in enumerate((ROWS - 1, 0)):
        w0, w1 = encode(*(column[t, 8 + 16 * k : 24 + 16 * k, :] for k in range(3)), axis=0)
        side_out[i, 0:16, :] = w0
        side_out[i, 16:32, :] = w1

    def side_copy(sem, target):
        return pltpu.make_async_remote_copy(
            src_ref=side_out.at[sem], dst_ref=side_in.at[sem], send_sem=send_sem.at[sem + 6],
            recv_sem=side_sem.at[sem], device_id={"grp": target}, device_id_type=MESH)

    up2 = side_copy(0, g + 1)
    down2 = side_copy(1, g - 1)

    @pl.when(g < 7)
    def _():
        up2.start()

    @pl.when(g > 0)
    def _():
        down2.start()

    for s in range(2):
        at_end = me == s * (COLS - 1)
        for t in range(ROWS):
            cell = cell_ref[s, t]
            d = dir_ref[s, t]
            r = lax.div(cell, NPH)
            c = jnp.clip(cell - r * NPH - s * (NPH - PHD), 0, PHD - 2)
            own = s * (PHD - 1)
            row1 = jnp.where(at_end, r, t)
            row2 = jnp.where(at_end, r + d, t)
            col1 = jnp.where(at_end, c, own)
            col2 = jnp.where(at_end, c + 1 - d, own)
            edge_out[s, pl.ds(t, 1), :] = 0.5 * (
                column[row1, pl.ds(col1 + 8, 1), :] + column[row2, pl.ds(col2 + 8, 1), :])
    edge_copies = []
    for s in range(2):
        at_end = me == s * (COLS - 1)
        there = jnp.where(at_end, me, me + 2 * s - 1)
        panel = jnp.where(at_end, 1 - p, p)
        slot = jnp.where(at_end, s, 1 - s)
        copy = pltpu.make_async_remote_copy(
            src_ref=edge_out.at[s], dst_ref=edge_in.at[slot], send_sem=send_sem.at[8 + s], recv_sem=edge_sem.at[slot],
            device_id={"panel": panel, "col": there}, device_id_type=MESH)
        copy.start()
        edge_copies.append(copy)

    def unpack_side(i):
        for k, part in enumerate(decode(side_in[i, 0:16, :], side_in[i, 16:32, :])):
            side[i, 16 * k : 16 * (k + 1), :] = part

    arrived(vel_in, first_part, vela_sem)
    arrived(vel_in, second_part, velb_sem)
    for i in range(3):
        vel_col[pl.ds(128 * i, 128), :] = jnp.transpose(vel_in[:, :, 128 * i : 128 * (i + 1)].reshape(NR, 128))

    for s in range(2):
        pltpu.make_async_copy(edge_in.at[s], edge_in.at[s], edge_sem.at[s]).wait()
    for t in range(ROWS):
        column[t, pl.ds(7, 1), :] = edge_in[0, pl.ds(t, 1), :]
        column[t, pl.ds(8 + PHD, 1), :] = edge_in[1, pl.ds(t, 1), :]

    def column_star(place):
        t = ORDER[place]
        center = column[t, inner, :]
        south = column[t - 1, inner, :] if t > 0 else side[0]
        north = column[t + 1, inner, :] if t < ROWS - 1 else side[1]
        east = column[t, pl.ds(9, PHD), :]
        west = column[t, pl.ds(7, PHD), :]
        half_t, half_p = half_vel(vel_col[pl.ds(place * PHD, PHD), :])
        star_col[pl.ds(place * PHD, PHD), :] = (
            center + KAPPA * (north + south + east + west - 4.0 * center)
            - half_t * (north - south) - half_p * (east - west)
        )

    matrix_halves = mat_h[...], mat_l[...]
    for place in range(6):
        column_star(place)
    solved[:, 0:256] = dot3(matrix_halves, halves(star_col[0:256]), ((1,), (1,)))

    def back_early_group(i, carry):
        q = lax.rem(own_group + i, GROUPS)
        rows = pl.ds(pl.multiple_of(q * 64, 64), 64)
        word, k = encode_early(solved[rows, 0:128], solved[rows, 128:256])
        back_early_out[pl.ds(q * 8, 8)] = word.reshape(8, LEV, 128)
        scales[rows, :] = k
        scatter_group(back_early_out, back_early_in, q, send_sem.at[10], back_early_sem.at[own_group])
        return carry

    lax.fori_loop(0, GROUPS, back_early_group, 0)

    @pl.when(g > 0)
    def _():
        up2.wait_recv()
        unpack_side(0)

    @pl.when(g < 7)
    def _():
        down2.wait_recv()
        unpack_side(1)

    column_star(6)
    column_star(7)
    solved[:, 256:384] = dot3(matrix_halves, halves(star_col[256:384]), ((1,), (1,)))

    def back_late_group(i, carry):
        q = lax.rem(own_group + i, GROUPS)
        rows = pl.ds(pl.multiple_of(q * 64, 64), 64)
        word = encode_late(solved[rows, 256:384], scales[rows, :])
        back_late_out[pl.ds(q * 8, 8)] = word.reshape(8, LEV, 128)
        scatter_group(back_late_out, back_late_in, q, send_sem.at[12], back_late_sem.at[own_group])
        return carry

    lax.fori_loop(0, GROUPS, back_late_group, 0)

    @pl.when(g < 7)
    def _():
        up.wait_send()
        up2.wait_send()

    @pl.when(g > 0)
    def _():
        down.wait_send()
        down2.wait_send()

    ghost_copy.wait_send()
    for copy in edge_copies:
        copy.wait_send()
    sent(vel_out, first_part, send_sem.at[3])
    sent(early_out, None, send_sem.at[4])
    sent(late_out, None, send_sem.at[11])
    sent(vel_out, second_part, send_sem.at[5])

    def out_group(i, carry):
        q = lax.rem(own_group + GROUPS - i, GROUPS)
        for part, sem in ((back_early_in, back_early_sem), (back_late_in, back_late_sem)):
            part = part.at[pl.ds(q * 8, 8)]
            pltpu.make_async_copy(part, part, sem.at[q]).wait()
        rows = []
        for d in range(8):
            rows.append(jnp.concatenate(decode_tiles(back_early_in[q * 8 + d], back_late_in[q * 8 + d]), axis=1))
        for t, row in zip(ORDER, swap_chunks(rows)):
            for k in range(3):
                tiles[q * 3 + k, pl.ds(t, LEV, stride=ROWS), :] = row[:, 128 * k : 128 * (k + 1)]
        for k in range(3):
            lanes = pl.ds(pl.multiple_of(q * CELLS + 128 * k, 128), 128)
            pltpu.make_async_copy(tiles.at[q * 3 + k], out_ref.at[:, lanes], load_sem.at[4]).start()
        return carry

    lax.fori_loop(0, GROUPS, out_group, 0)
    pltpu.make_async_copy(tiles, tiles, load_sem.at[4]).wait()
    sent(back_early_out, None, send_sem.at[10])
    sent(back_late_out, None, send_sem.at[12])


def per_device(field, vel_theta, vel_phi, strip_cell, strip_dir, radial_inverse):
    smem = pl.BlockSpec(memory_space=pltpu.SMEM)
    hbm = pl.BlockSpec(memory_space=pl.ANY)
    flat = (LEV * ROWS, NPH)
    tiled = (TILES, LEV * ROWS, 128)
    dma = pltpu.SemaphoreType.DMA
    out = pl.pallas_call(
        kernel,
        out_shape=jax.ShapeDtypeStruct(flat, F32),
        in_specs=[smem, smem, hbm, hbm, hbm, hbm],
        out_specs=pl.BlockSpec(memory_space=pltpu.VMEM),
        scratch_shapes=[
            pltpu.VMEM(tiled, F32), pltpu.VMEM(flat, BF16), pltpu.VMEM(flat, BF16), pltpu.VMEM((NR, NR), F32),
            pltpu.VMEM((NR, NR), BF16), pltpu.VMEM((NR, NR), BF16), pltpu.VMEM((NR, NR), BF16), pltpu.VMEM((NR, NR), BF16),
            pltpu.VMEM((ROWS, LEV, NPH), F32), pltpu.VMEM((2, LEV, 1024), I32), pltpu.VMEM((2, LEV, 1024), I32), pltpu.VMEM((2, LEV, NPH), F32), pltpu.VMEM(tiled, I32), pltpu.VMEM((ROWS, LEV, NPH), F32),
            pltpu.VMEM((LEV, 128), F32), pltpu.VMEM((LEV, 128), F32),
            pltpu.VMEM((COLS, LEV, CELLS), I32), pltpu.VMEM((COLS, LEV, CELLS), I32),
            *[pltpu.VMEM((COLS, LEV, 128), I32)] * 8, pltpu.VMEM((NR, 128), I32),
            pltpu.VMEM((ROWS, 64, NR), F32), pltpu.VMEM((2, 32, NR), I32), pltpu.VMEM((2, 32, NR), I32), pltpu.VMEM((2, PHD, NR), F32),
            pltpu.VMEM((2, ROWS, NR), F32), pltpu.VMEM((2, ROWS, NR), F32),
            pltpu.VMEM((CELLS, NR), I32), pltpu.VMEM((CELLS, NR), F32), pltpu.VMEM((NR, CELLS), F32), pltpu.VMEM(tiled, F32),
            dma((5,)), dma((13,)), dma((2,)), dma, dma, dma, dma, dma,
            dma((GROUPS,)), dma((GROUPS,)), dma((2,)), dma((2,)),
        ],
        compiler_params=pltpu.CompilerParams(
            collective_id=0, has_side_effects=True, vmem_limit_bytes=60 * 2**20),
    )(
        strip_cell[0].T, strip_dir[0].T, field.reshape(flat), vel_theta.reshape(flat), vel_phi.reshape(flat),
        radial_inverse,
    )
    return out.reshape(1, LEV, ROWS, NPH)


def solution(mesh):
    placed = (
        P("panel", "col", "grp", None),
        P("panel", "col", "grp", None),
        P("panel", "col", "grp", None),
        P("panel", "grp", None),
        P("panel", "grp", None),
        P(),
    )
    return jax.shard_map(
        per_device, mesh=mesh, in_specs=placed, out_specs=P("panel", "col", "grp", None), check_vma=False)
```

```python
import functools

import jax
import jax.numpy as jnp
from jax import lax
from jax.experimental import pallas as pl
from jax.experimental.pallas import tpu as pltpu
from jax.sharding import PartitionSpec as P

MESH = pl.DeviceIdType.MESH
KAPPA = 0.2
COLS = 32
LEV = 8
ROWS = 8
NPH = 1536
PHD = 48
NR = 256
CELLS = ROWS * PHD
GROUPS = NPH // CELLS
TILES = NPH // 128
VEL_ONE = 32767.0
ORDER = (1, 2, 3, 4, 5, 6, 0, 7)
F32 = jnp.float32
I32 = jnp.int32
BF16 = jnp.bfloat16


def to_int(x):
    return (x + jnp.where(x >= 0.0, 0.5, -0.5)).astype(I32)


def pack_vel(vt, vp):
    qt = to_int(vt.astype(F32) * VEL_ONE)
    qp = to_int(vp.astype(F32) * VEL_ONE)
    return (qt & 0xFFFF) | (qp << 16)


def half_vel(word):
    scale = 0.5 / VEL_ONE
    return ((word << 16) >> 16).astype(F32) * scale, (word >> 16).astype(F32) * scale


def swap_chunks(rows):
    lane = lax.broadcasted_iota(I32, rows[0].shape, 1)
    chunk = (lane * 1366) >> 16
    rows = list(rows)
    for bit in (1, 2, 4):
        inside = (chunk & bit) != 0
        for low in range(8):
            if low & bit:
                continue
            a, b = rows[low], rows[low | bit]
            rows[low] = jnp.where(inside, pltpu.roll(b, PHD * bit, 1), a)
            rows[low | bit] = jnp.where(inside, b, pltpu.roll(a, CELLS - PHD * bit, 1))
    return rows


def encode(x0, x1, x2, axis=1):
    top = jnp.maximum(jnp.maximum(jnp.abs(x0), jnp.abs(x1)), jnp.abs(x2))
    top = jnp.max(top, axis=axis, keepdims=True)
    top = jnp.broadcast_to(jnp.maximum(top, 1e-30), x0.shape)
    k = jnp.ceil(jnp.log2(top) * 4.0).astype(I32) + (1 - 4 * 17)
    inverse = jnp.exp2(k.astype(F32) * -0.25)
    q0, q1, q2 = (to_int(x * inverse) for x in (x0, x1, x2))
    return (
        (q0 << 14) | ((q1 >> 4) & 0x3FFF),
        (q2 << 14) | ((q1 & 15) << 10) | (k & 0x3FF),
    )


def decode(w0, w1):
    scale = jnp.exp2(((w1 << 22) >> 22).astype(F32) * 0.25)
    q1 = (((w0 << 18) >> 18) << 4) | ((w1 >> 10) & 15)
    return (
        (w0 >> 14).astype(F32) * scale,
        q1.astype(F32) * scale,
        (w1 >> 14).astype(F32) * scale,
    )


def scale_code(top, bits):
    top = jnp.maximum(jnp.max(top, axis=1, keepdims=True), 1e-30)
    return jnp.ceil(jnp.log2(jnp.broadcast_to(top, (top.shape[0], 128))) * 4.0).astype(I32) + (1 - 4 * bits)


def quarter_power(k):
    return jnp.exp2(k.astype(F32) * 0.25)


def encode_early(x0, x1):
    k = scale_code(jnp.maximum(jnp.abs(x0), jnp.abs(x1)), 15)
    inverse = quarter_power(-k)
    return (to_int(x0 * inverse) & 0xFFFF) | (to_int(x1 * inverse) << 16), k


def encode_late(x, early):
    k = scale_code(jnp.abs(x), 19)
    lane = lax.broadcasted_iota(I32, x.shape, 1)
    return (to_int(x * quarter_power(-k)) << 12) | (jnp.where(lane < 64, early, k) & 0xFFF)


def decode_tiles(early, late):
    k = (late << 20) >> 20
    scale_early = jnp.broadcast_to(quarter_power(k[:, 0:1]), late.shape)
    scale_late = jnp.broadcast_to(quarter_power(k[:, 127:128]), late.shape)
    return (
        ((early << 16) >> 16).astype(F32) * scale_early,
        (early >> 16).astype(F32) * scale_early,
        (late >> 12).astype(F32) * scale_late,
    )


def halves(x):
    high = x.astype(BF16)
    return high, (x - high.astype(F32)).astype(BF16)


def dot3(a, b, dims):
    ah, al = a
    bh, bl = b
    mul = functools.partial(lax.dot_general, dimension_numbers=(dims, ((), ())), preferred_element_type=F32)
    return mul(ah, bh) + (mul(ah, bl) + mul(al, bh))


def kernel(
    cell_ref, dir_ref, field_hbm, vt_hbm, vp_hbm, mat_hbm,
    out_ref,
    field, vt, vp, mat, mat_h, mat_l, tmat_h, tmat_l,
    state, row_out, row_in, halo, words, star, ghost_out, ghost_in,
    vel_out, vel_in, early_out, early_in, late_out, late_in,
    back_early_out, back_early_in, back_late_out, back_late_in, scales,
    column, side_out, side_in, side, edge_out, edge_in, vel_col, star_col, solved, tiles,
    load_sem, send_sem, row_sem, ghost_sem, vela_sem, velb_sem, velc_sem, early_sem, late_sem,
    back_early_sem, back_late_sem, side_sem, edge_sem,
):
    p = lax.axis_index("panel")
    g = lax.axis_index("grp")
    me = lax.axis_index("col")

    for k in range(TILES):
        pltpu.make_async_copy(field_hbm.at[:, pl.ds(128 * k, 128)], field.at[k], load_sem.at[0]).start()
    loads = [
        pltpu.make_async_copy(src, dst, load_sem.at[i])
        for i, (src, dst) in enumerate(((field, field), (vt_hbm, vt), (vp_hbm, vp), (mat_hbm, mat)))
    ]
    for copy in loads[1:]:
        copy.start()

    barrier = pltpu.get_barrier_semaphore()

    def greet(s, carry):
        pl.semaphore_signal(barrier, inc=1, device_id={"col": lax.rem(me + s, COLS)}, device_id_type=MESH)
        return carry

    lax.fori_loop(1, COLS, greet, 0)
    pl.semaphore_signal(barrier, inc=1, device_id={"panel": 1 - p}, device_id_type=MESH)

    @pl.when(g > 0)
    def _():
        pl.semaphore_signal(barrier, inc=1, device_id={"grp": g - 1}, device_id_type=MESH)

    @pl.when(g < 7)
    def _():
        pl.semaphore_signal(barrier, inc=1, device_id={"grp": g + 1}, device_id_type=MESH)

    loads[0].wait()
    for t in range(ROWS):
        for k in range(TILES):
            lanes = pl.ds(128 * k, 128)
            state[t, :, lanes] = field[k, pl.ds(t, LEV, stride=ROWS), :]

    @pl.when(g == 0)
    def _():
        halo[0] = jnp.zeros((LEV, NPH), F32)

    @pl.when(g == 7)
    def _():
        halo[1] = jnp.zeros((LEV, NPH), F32)

    for i, t in enumerate((ROWS - 1, 0)):
        for q in range(GROUPS):
            w0, w1 = encode(*(state[t, :, CELLS * q + 128 * k : CELLS * q + 128 * (k + 1)] for k in range(3)))
            row_out[i, :, 256 * q : 256 * q + 128] = w0
            row_out[i, :, 256 * q + 128 : 256 * (q + 1)] = w1

    count = COLS + jnp.where(g > 0, 1, 0) + jnp.where(g < 7, 1, 0)
    pl.semaphore_wait(barrier, count)

    def row_copy(sem, target):
        return pltpu.make_async_remote_copy(
            src_ref=row_out.at[sem], dst_ref=row_in.at[sem], send_sem=send_sem.at[sem], recv_sem=row_sem.at[sem],
            device_id={"grp": target}, device_id_type=MESH)

    up = row_copy(0, g + 1)
    down = row_copy(1, g - 1)

    @pl.when(g < 7)
    def _():
        up.start()

    @pl.when(g > 0)
    def _():
        down.start()

    lane = lax.broadcasted_iota(I32, (LEV, 128), 1)
    ghosts = jnp.zeros((LEV, 128), F32)
    for t in range(ROWS):
        for s in range(2):
            cell = cell_ref[s, t]
            d = dir_ref[s, t]
            r = lax.div(cell, NPH)
            c = cell - r * NPH - s * (NPH - 128)
            lanes = pl.ds(s * (NPH - 128), 128)
            first = state[r, :, lanes]
            second = state[r + d, :, lanes]
            both = jnp.where(lane == c, first, 0.0) + jnp.where(lane == c + 1 - d, second, 0.0)
            value = 0.5 * jnp.sum(both, axis=1, keepdims=True)
            ghosts = jnp.where(lane == 2 * t + s, value, ghosts)
    ghost_out[...] = ghosts

    ghost_copy = pltpu.make_async_remote_copy(
        src_ref=ghost_out, dst_ref=ghost_in, send_sem=send_sem.at[2], recv_sem=ghost_sem,
        device_id={"panel": 1 - p}, device_id_type=MESH)
    ghost_copy.start()

    loads[1].wait()
    loads[2].wait()
    for k in range(TILES):
        words[k] = pack_vel(vt[:, 128 * k : 128 * (k + 1)], vp[:, 128 * k : 128 * (k + 1)])

    def vel_group(q, carry):
        rows = []
        for t in ORDER:
            parts = [words[q * 3 + k, pl.ds(t, LEV, stride=ROWS), :] for k in range(3)]
            rows.append(jnp.concatenate(parts, axis=1))
        for d, row in enumerate(swap_chunks(rows)):
            vel_out[q * 8 + d] = row
        return carry

    lax.fori_loop(0, GROUPS, vel_group, 0)

    def scatter(src, dst, lanes, send, recv):
        def part(ref, i):
            return ref.at[i] if lanes is None else ref.at[i, :, lanes]

        def one(s, carry):
            d = lax.rem(me + s, COLS)
            pltpu.make_async_remote_copy(
                src_ref=part(src, d), dst_ref=part(dst, me), send_sem=send, recv_sem=recv,
                device_id={"col": d}, device_id_type=MESH).start()
            return carry

        lax.fori_loop(1, COLS, one, 0)
        pltpu.make_async_copy(part(src, me), part(dst, me), recv).start()

    def scatter_group(src, dst, q, send, recv):
        for j in range(8):
            d = q * 8 + j

            @pl.when(d != me)
            def _():
                pltpu.make_async_remote_copy(
                    src_ref=src.at[d], dst_ref=dst.at[me], send_sem=send, recv_sem=recv,
                    device_id={"col": d}, device_id_type=MESH).start()

            @pl.when(d == me)
            def _():
                pltpu.make_async_copy(src.at[d], dst.at[d], recv).start()

    own_group = lax.div(me, 8)

    def arrived(dst, lanes, recv):
        whole = dst if lanes is None else dst.at[:, :, lanes]
        pltpu.make_async_copy(whole, whole, recv).wait()

    def sent(src, lanes, send):
        most = src.at[pl.ds(0, COLS - 1)] if lanes is None else src.at[pl.ds(0, COLS - 1), :, lanes]
        pltpu.make_async_copy(most, most, send).wait()

    first_part, second_part, third_part = (pl.ds(128 * i, 128) for i in range(3))
    scatter(vel_out, vel_in, first_part, send_sem.at[3], vela_sem)

    ghost_copy.wait_recv()

    wide = lax.broadcasted_iota(I32, (LEV, NPH), 1)
    ghosts = ghost_in[...]

    def star_row(place):
        t = ORDER[place]
        center = state[t]
        south = state[t - 1] if t > 0 else halo[0]
        north = state[t + 1] if t < ROWS - 1 else halo[1]
        west = jnp.where(wide == 0, ghosts[:, 2 * t : 2 * t + 1], pltpu.roll(center, 1, 1))
        east = jnp.where(wide == NPH - 1, ghosts[:, 2 * t + 1 : 2 * t + 2], pltpu.roll(center, NPH - 1, 1))
        word = jnp.concatenate(
            [words[k, pl.ds(t, LEV, stride=ROWS), :] for k in range(TILES)], axis=1)
        half_t, half_p = half_vel(word)
        star[place] = (
            center + KAPPA * (north + south + east + west - 4.0 * center)
            - half_t * (north - south) - half_p * (east - west)
        )

    for place in range(6):
        star_row(place)

    def early_group(i, carry):
        q = lax.rem(own_group + i, GROUPS)
        lanes = pl.ds(pl.multiple_of(q * CELLS, 128), CELLS)
        rows = swap_chunks([star[place if place < 6 else 0, :, lanes] for place in range(ROWS)])
        for d, row in enumerate(rows):
            word, k = encode_early(row[:, 0:128], row[:, 128:256])
            early_out[q * 8 + d] = word
            scales[pl.ds(pl.multiple_of(q * 64 + 8 * d, 8), 8), :] = k
        scatter_group(early_out, early_in, q, send_sem.at[4], early_sem)
        return carry

    lax.fori_loop(0, GROUPS, early_group, 0)

    def unpack_row(i):
        for q in range(GROUPS):
            parts = decode(row_in[i, :, 256 * q : 256 * q + 128], row_in[i, :, 256 * q + 128 : 256 * (q + 1)])
            for k, part in enumerate(parts):
                halo[i, :, CELLS * q + 128 * k : CELLS * q + 128 * (k + 1)] = part

    @pl.when(g > 0)
    def _():
        up.wait_recv()
        unpack_row(0)

    @pl.when(g < 7)
    def _():
        down.wait_recv()
        unpack_row(1)

    star_row(6)
    star_row(7)

    def late_group(i, carry):
        q = lax.rem(own_group + i, GROUPS)
        lanes = pl.ds(pl.multiple_of(q * CELLS, 128), CELLS)
        rows = swap_chunks([star[place, :, lanes] for place in range(ROWS)])
        for d, row in enumerate(rows):
            k = scales[pl.ds(pl.multiple_of(q * 64 + 8 * d, 8), 8), :]
            late_out[q * 8 + d] = encode_late(row[:, 256:384], k)
        scatter_group(late_out, late_in, q, send_sem.at[11], late_sem)
        return carry

    lax.fori_loop(0, GROUPS, late_group, 0)
    loads[3].wait()
    matrix = mat[...]
    mat_h[...], mat_l[...] = halves(matrix)
    tmat_h[...], tmat_l[...] = halves(jnp.transpose(matrix))

    sent(early_out, None, send_sem.at[4])
    sent(late_out, None, send_sem.at[11])
    scatter(vel_out, vel_in, second_part, send_sem.at[5], velb_sem)
    arrived(early_in, None, early_sem)
    arrived(late_in, None, late_sem)
    scatter(vel_out, vel_in, third_part, send_sem.at[13], velc_sem)
    tiles1 = decode_tiles(early_in[...].reshape(NR, 128), late_in[...].reshape(NR, 128))
    for i, tile in enumerate(tiles1):
        star_col[pl.ds(128 * i, 128), :] = jnp.transpose(tile)
    first = dot3(halves(star_col[...]), (tmat_h[...], tmat_l[...]), ((1,), (0,)))
    for place, t in enumerate(ORDER):
        column[t, pl.ds(8, PHD), :] = first[place * PHD : (place + 1) * PHD]

    @pl.when(g == 0)
    def _():
        side[0] = jnp.zeros((PHD, NR), F32)

    @pl.when(g == 7)
    def _():
        side[1] = jnp.zeros((PHD, NR), F32)

    inner = pl.ds(8, PHD)
    for i, t in enumerate((ROWS - 1, 0)):
        w0, w1 = encode(*(column[t, 8 + 16 * k : 24 + 16 * k, :] for k in range(3)), axis=0)
        side_out[i, 0:16, :] = w0
        side_out[i, 16:32, :] = w1

    def side_copy(sem, target):
        return pltpu.make_async_remote_copy(
            src_ref=side_out.at[sem], dst_ref=side_in.at[sem], send_sem=send_sem.at[sem + 6],
            recv_sem=side_sem.at[sem], device_id={"grp": target}, device_id_type=MESH)

    up2 = side_copy(0, g + 1)
    down2 = side_copy(1, g - 1)

    @pl.when(g < 7)
    def _():
        up2.start()

    @pl.when(g > 0)
    def _():
        down2.start()

    for s in range(2):
        at_end = me == s * (COLS - 1)
        for t in range(ROWS):
            cell = cell_ref[s, t]
            d = dir_ref[s, t]
            r = lax.div(cell, NPH)
            c = jnp.clip(cell - r * NPH - s * (NPH - PHD), 0, PHD - 2)
            own = s * (PHD - 1)
            row1 = jnp.where(at_end, r, t)
            row2 = jnp.where(at_end, r + d, t)
            col1 = jnp.where(at_end, c, own)
            col2 = jnp.where(at_end, c + 1 - d, own)
            edge_out[s, pl.ds(t, 1), :] = 0.5 * (
                column[row1, pl.ds(col1 + 8, 1), :] + column[row2, pl.ds(col2 + 8, 1), :])
    edge_copies = []
    for s in range(2):
        at_end = me == s * (COLS - 1)
        there = jnp.where(at_end, me, me + 2 * s - 1)
        panel = jnp.where(at_end, 1 - p, p)
        slot = jnp.where(at_end, s, 1 - s)
        copy = pltpu.make_async_remote_copy(
            src_ref=edge_out.at[s], dst_ref=edge_in.at[slot], send_sem=send_sem.at[8 + s], recv_sem=edge_sem.at[slot],
            device_id={"panel": panel, "col": there}, device_id_type=MESH)
        copy.start()
        edge_copies.append(copy)

    def unpack_side(i):
        for k, part in enumerate(decode(side_in[i, 0:16, :], side_in[i, 16:32, :])):
            side[i, 16 * k : 16 * (k + 1), :] = part

    def turn(i):
        vel_col[pl.ds(128 * i, 128), :] = jnp.transpose(vel_in[:, :, 128 * i : 128 * (i + 1)].reshape(NR, 128))

    arrived(vel_in, first_part, vela_sem)
    arrived(vel_in, second_part, velb_sem)
    turn(0)
    turn(1)

    for s in range(2):
        pltpu.make_async_copy(edge_in.at[s], edge_in.at[s], edge_sem.at[s]).wait()
    for t in range(ROWS):
        column[t, pl.ds(7, 1), :] = edge_in[0, pl.ds(t, 1), :]
        column[t, pl.ds(8 + PHD, 1), :] = edge_in[1, pl.ds(t, 1), :]

    def column_star(place, start=0, size=PHD):
        t = ORDER[place]
        part = pl.ds(8 + start, size)
        center = column[t, part, :]
        south = column[t - 1, part, :] if t > 0 else side[0]
        north = column[t + 1, part, :] if t < ROWS - 1 else side[1]
        east = column[t, pl.ds(9 + start, size), :]
        west = column[t, pl.ds(7 + start, size), :]
        half_t, half_p = half_vel(vel_col[pl.ds(place * PHD + start, size), :])
        star_col[pl.ds(place * PHD + start, size), :] = (
            center + KAPPA * (north + south + east + west - 4.0 * center)
            - half_t * (north - south) - half_p * (east - west)
        )

    matrix_halves = mat_h[...], mat_l[...]
    for place in range(5):
        column_star(place)
    column_star(5, 0, 16)
    solved[:, 0:256] = dot3(matrix_halves, halves(star_col[0:256]), ((1,), (1,)))

    def back_early_group(i, carry):
        q = lax.rem(own_group + i, GROUPS)
        rows = pl.ds(pl.multiple_of(q * 64, 64), 64)
        word, k = encode_early(solved[rows, 0:128], solved[rows, 128:256])
        back_early_out[pl.ds(q * 8, 8)] = word.reshape(8, LEV, 128)
        scales[rows, :] = k
        scatter_group(back_early_out, back_early_in, q, send_sem.at[10], back_early_sem.at[own_group])
        return carry

    lax.fori_loop(0, GROUPS, back_early_group, 0)

    arrived(vel_in, third_part, velc_sem)
    turn(2)
    column_star(5, 16, 32)

    @pl.when(g > 0)
    def _():
        up2.wait_recv()
        unpack_side(0)

    @pl.when(g < 7)
    def _():
        down2.wait_recv()
        unpack_side(1)

    column_star(6)
    column_star(7)
    solved[:, 256:384] = dot3(matrix_halves, halves(star_col[256:384]), ((1,), (1,)))

    def back_late_group(i, carry):
        q = lax.rem(own_group + i, GROUPS)
        rows = pl.ds(pl.multiple_of(q * 64, 64), 64)
        word = encode_late(solved[rows, 256:384], scales[rows, :])
        back_late_out[pl.ds(q * 8, 8)] = word.reshape(8, LEV, 128)
        scatter_group(back_late_out, back_late_in, q, send_sem.at[12], back_late_sem.at[own_group])
        return carry

    lax.fori_loop(0, GROUPS, back_late_group, 0)

    @pl.when(g < 7)
    def _():
        up.wait_send()
        up2.wait_send()

    @pl.when(g > 0)
    def _():
        down.wait_send()
        down2.wait_send()

    ghost_copy.wait_send()
    for copy in edge_copies:
        copy.wait_send()
    sent(vel_out, first_part, send_sem.at[3])
    sent(vel_out, second_part, send_sem.at[5])
    sent(vel_out, third_part, send_sem.at[13])

    def out_group(i, carry):
        q = lax.rem(own_group + GROUPS - i, GROUPS)
        for part, sem in ((back_early_in, back_early_sem), (back_late_in, back_late_sem)):
            part = part.at[pl.ds(q * 8, 8)]
            pltpu.make_async_copy(part, part, sem.at[q]).wait()
        rows = []
        for d in range(8):
            rows.append(jnp.concatenate(decode_tiles(back_early_in[q * 8 + d], back_late_in[q * 8 + d]), axis=1))
        for t, row in zip(ORDER, swap_chunks(rows)):
            for k in range(3):
                tiles[q * 3 + k, pl.ds(t, LEV, stride=ROWS), :] = row[:, 128 * k : 128 * (k + 1)]
        for k in range(3):
            lanes = pl.ds(pl.multiple_of(q * CELLS + 128 * k, 128), 128)
            pltpu.make_async_copy(tiles.at[q * 3 + k], out_ref.at[:, lanes], load_sem.at[4]).start()
        return carry

    lax.fori_loop(0, GROUPS, out_group, 0)
    pltpu.make_async_copy(tiles, tiles, load_sem.at[4]).wait()
    sent(back_early_out, None, send_sem.at[10])
    sent(back_late_out, None, send_sem.at[12])


def per_device(field, vel_theta, vel_phi, strip_cell, strip_dir, radial_inverse):
    smem = pl.BlockSpec(memory_space=pltpu.SMEM)
    hbm = pl.BlockSpec(memory_space=pl.ANY)
    flat = (LEV * ROWS, NPH)
    tiled = (TILES, LEV * ROWS, 128)
    dma = pltpu.SemaphoreType.DMA
    out = pl.pallas_call(
        kernel,
        out_shape=jax.ShapeDtypeStruct(flat, F32),
        in_specs=[smem, smem, hbm, hbm, hbm, hbm],
        out_specs=pl.BlockSpec(memory_space=pl.ANY),
        scratch_shapes=[
            pltpu.VMEM(tiled, F32), pltpu.VMEM(flat, BF16), pltpu.VMEM(flat, BF16), pltpu.VMEM((NR, NR), F32),
            pltpu.VMEM((NR, NR), BF16), pltpu.VMEM((NR, NR), BF16), pltpu.VMEM((NR, NR), BF16), pltpu.VMEM((NR, NR), BF16),
            pltpu.VMEM((ROWS, LEV, NPH), F32), pltpu.VMEM((2, LEV, 1024), I32), pltpu.VMEM((2, LEV, 1024), I32), pltpu.VMEM((2, LEV, NPH), F32), pltpu.VMEM(tiled, I32), pltpu.VMEM((ROWS, LEV, NPH), F32),
            pltpu.VMEM((LEV, 128), F32), pltpu.VMEM((LEV, 128), F32),
            pltpu.VMEM((COLS, LEV, CELLS), I32), pltpu.VMEM((COLS, LEV, CELLS), I32),
            *[pltpu.VMEM((COLS, LEV, 128), I32)] * 8, pltpu.VMEM((NR, 128), I32),
            pltpu.VMEM((ROWS, 64, NR), F32), pltpu.VMEM((2, 32, NR), I32), pltpu.VMEM((2, 32, NR), I32), pltpu.VMEM((2, PHD, NR), F32),
            pltpu.VMEM((2, ROWS, NR), F32), pltpu.VMEM((2, ROWS, NR), F32),
            pltpu.VMEM((CELLS, NR), I32), pltpu.VMEM((CELLS, NR), F32), pltpu.VMEM((NR, CELLS), F32), pltpu.VMEM(tiled, F32),
            dma((5,)), dma((14,)), dma((2,)), dma, dma, dma, dma, dma, dma,
            dma((GROUPS,)), dma((GROUPS,)), dma((2,)), dma((2,)),
        ],
        compiler_params=pltpu.CompilerParams(
            collective_id=0, has_side_effects=True, vmem_limit_bytes=60 * 2**20),
    )(
        strip_cell[0].T, strip_dir[0].T, field.reshape(flat), vel_theta.reshape(flat), vel_phi.reshape(flat),
        radial_inverse,
    )
    return out.reshape(1, LEV, ROWS, NPH)


def solution(mesh):
    placed = (
        P("panel", "col", "grp", None),
        P("panel", "col", "grp", None),
        P("panel", "col", "grp", None),
        P("panel", "grp", None),
        P("panel", "grp", None),
        P(),
    )
    return jax.shard_map(
        per_device, mesh=mesh, in_specs=placed, out_specs=P("panel", "col", "grp", None), check_vma=False)
```

```python
import functools

import jax
import jax.numpy as jnp
from jax import lax
from jax.experimental import pallas as pl
from jax.experimental.pallas import tpu as pltpu
from jax.sharding import PartitionSpec as P

MESH = pl.DeviceIdType.MESH
KAPPA = 0.2
COLS = 32
LEV = 8
ROWS = 8
NPH = 1536
PHD = 48
NR = 256
CELLS = ROWS * PHD
GROUPS = NPH // CELLS
TILES = NPH // 128
VEL_ONE = 32767.0
ORDER = (1, 2, 3, 4, 5, 6, 0, 7)
F32 = jnp.float32
I32 = jnp.int32
BF16 = jnp.bfloat16


def to_int(x):
    return (x + jnp.where(x >= 0.0, 0.5, -0.5)).astype(I32)


def pack_vel(vt, vp):
    qt = to_int(vt.astype(F32) * VEL_ONE)
    qp = to_int(vp.astype(F32) * VEL_ONE)
    return (qt & 0xFFFF) | (qp << 16)


def half_vel(word):
    scale = 0.5 / VEL_ONE
    return ((word << 16) >> 16).astype(F32) * scale, (word >> 16).astype(F32) * scale


def swap_chunks(rows):
    lane = lax.broadcasted_iota(I32, rows[0].shape, 1)
    chunk = (lane * 1366) >> 16
    rows = list(rows)
    for bit in (1, 2, 4):
        inside = (chunk & bit) != 0
        for low in range(8):
            if low & bit:
                continue
            a, b = rows[low], rows[low | bit]
            rows[low] = jnp.where(inside, pltpu.roll(b, PHD * bit, 1), a)
            rows[low | bit] = jnp.where(inside, b, pltpu.roll(a, CELLS - PHD * bit, 1))
    return rows


def encode(x0, x1, x2, axis=1):
    top = jnp.maximum(jnp.maximum(jnp.abs(x0), jnp.abs(x1)), jnp.abs(x2))
    top = jnp.max(top, axis=axis, keepdims=True)
    top = jnp.broadcast_to(jnp.maximum(top, 1e-30), x0.shape)
    k = jnp.ceil(jnp.log2(top) * 4.0).astype(I32) + (1 - 4 * 17)
    inverse = jnp.exp2(k.astype(F32) * -0.25)
    q0, q1, q2 = (to_int(x * inverse) for x in (x0, x1, x2))
    return (
        (q0 << 14) | ((q1 >> 4) & 0x3FFF),
        (q2 << 14) | ((q1 & 15) << 10) | (k & 0x3FF),
    )


def decode(w0, w1):
    scale = jnp.exp2(((w1 << 22) >> 22).astype(F32) * 0.25)
    q1 = (((w0 << 18) >> 18) << 4) | ((w1 >> 10) & 15)
    return (
        (w0 >> 14).astype(F32) * scale,
        q1.astype(F32) * scale,
        (w1 >> 14).astype(F32) * scale,
    )


def scale_code(top, bits):
    top = jnp.maximum(jnp.max(top, axis=1, keepdims=True), 1e-30)
    return jnp.ceil(jnp.log2(jnp.broadcast_to(top, (top.shape[0], 128))) * 4.0).astype(I32) + (1 - 4 * bits)


def quarter_power(k):
    return jnp.exp2(k.astype(F32) * 0.25)


def encode_early(x0, x1):
    k = scale_code(jnp.maximum(jnp.abs(x0), jnp.abs(x1)), 15)
    inverse = quarter_power(-k)
    return (to_int(x0 * inverse) & 0xFFFF) | (to_int(x1 * inverse) << 16), k


def encode_late(x, early):
    k = scale_code(jnp.abs(x), 19)
    lane = lax.broadcasted_iota(I32, x.shape, 1)
    return (to_int(x * quarter_power(-k)) << 12) | (jnp.where(lane < 64, early, k) & 0xFFF)


def decode_tiles(early, late):
    k = (late << 20) >> 20
    scale_early = jnp.broadcast_to(quarter_power(k[:, 0:1]), late.shape)
    scale_late = jnp.broadcast_to(quarter_power(k[:, 127:128]), late.shape)
    return (
        ((early << 16) >> 16).astype(F32) * scale_early,
        (early >> 16).astype(F32) * scale_early,
        (late >> 12).astype(F32) * scale_late,
    )


def halves(x):
    high = x.astype(BF16)
    return high, (x - high.astype(F32)).astype(BF16)


def dot3(a, b, dims):
    ah, al = a
    bh, bl = b
    mul = functools.partial(lax.dot_general, dimension_numbers=(dims, ((), ())), preferred_element_type=F32)
    return mul(ah, bh) + (mul(ah, bl) + mul(al, bh))


def kernel(
    cell_ref, dir_ref, field_hbm, vt_hbm, vp_hbm, mat_hbm,
    out_ref,
    field, vt, vp, mat, mat_h, mat_l, tmat_h, tmat_l,
    state, row_out, row_in, halo, words, star, ghost_out, ghost_in,
    vel_out, vel_in, early_out, early_in, late_out, late_in,
    back_out, back_in, scales,
    column, side_out, side_in, side, edge_out, edge_in, vel_col, star_col, solved, tiles,
    load_sem, send_sem, row_sem, ghost_sem, vela_sem, velb_sem, velc_sem, early_sem, late_sem,
    back_sem, side_sem, edge_sem,
):
    p = lax.axis_index("panel")
    g = lax.axis_index("grp")
    me = lax.axis_index("col")

    for k in range(TILES):
        pltpu.make_async_copy(field_hbm.at[:, pl.ds(128 * k, 128)], field.at[k], load_sem.at[0]).start()
    loads = [
        pltpu.make_async_copy(src, dst, load_sem.at[i])
        for i, (src, dst) in enumerate(((field, field), (vt_hbm, vt), (vp_hbm, vp), (mat_hbm, mat)))
    ]
    for copy in loads[1:]:
        copy.start()

    barrier = pltpu.get_barrier_semaphore()

    def greet(s, carry):
        pl.semaphore_signal(barrier, inc=1, device_id={"col": lax.rem(me + s, COLS)}, device_id_type=MESH)
        return carry

    lax.fori_loop(1, COLS, greet, 0)
    pl.semaphore_signal(barrier, inc=1, device_id={"panel": 1 - p}, device_id_type=MESH)

    @pl.when(g > 0)
    def _():
        pl.semaphore_signal(barrier, inc=1, device_id={"grp": g - 1}, device_id_type=MESH)

    @pl.when(g < 7)
    def _():
        pl.semaphore_signal(barrier, inc=1, device_id={"grp": g + 1}, device_id_type=MESH)

    loads[0].wait()
    for t in range(ROWS):
        for k in range(TILES):
            lanes = pl.ds(128 * k, 128)
            state[t, :, lanes] = field[k, pl.ds(t, LEV, stride=ROWS), :]

    @pl.when(g == 0)
    def _():
        halo[0] = jnp.zeros((LEV, NPH), F32)

    @pl.when(g == 7)
    def _():
        halo[1] = jnp.zeros((LEV, NPH), F32)

    for i, t in enumerate((ROWS - 1, 0)):
        for q in range(GROUPS):
            w0, w1 = encode(*(state[t, :, CELLS * q + 128 * k : CELLS * q + 128 * (k + 1)] for k in range(3)))
            row_out[i, :, 256 * q : 256 * q + 128] = w0
            row_out[i, :, 256 * q + 128 : 256 * (q + 1)] = w1

    count = COLS + jnp.where(g > 0, 1, 0) + jnp.where(g < 7, 1, 0)
    pl.semaphore_wait(barrier, count)

    def row_copy(sem, target):
        return pltpu.make_async_remote_copy(
            src_ref=row_out.at[sem], dst_ref=row_in.at[sem], send_sem=send_sem.at[sem], recv_sem=row_sem.at[sem],
            device_id={"grp": target}, device_id_type=MESH)

    up = row_copy(0, g + 1)
    down = row_copy(1, g - 1)

    @pl.when(g < 7)
    def _():
        up.start()

    @pl.when(g > 0)
    def _():
        down.start()

    lane = lax.broadcasted_iota(I32, (LEV, 128), 1)
    ghosts = jnp.zeros((LEV, 128), F32)
    for t in range(ROWS):
        for s in range(2):
            cell = cell_ref[s, t]
            d = dir_ref[s, t]
            r = lax.div(cell, NPH)
            c = cell - r * NPH - s * (NPH - 128)
            lanes = pl.ds(s * (NPH - 128), 128)
            first = state[r, :, lanes]
            second = state[r + d, :, lanes]
            both = jnp.where(lane == c, first, 0.0) + jnp.where(lane == c + 1 - d, second, 0.0)
            value = 0.5 * jnp.sum(both, axis=1, keepdims=True)
            ghosts = jnp.where(lane == 2 * t + s, value, ghosts)
    ghost_out[...] = ghosts

    ghost_copy = pltpu.make_async_remote_copy(
        src_ref=ghost_out, dst_ref=ghost_in, send_sem=send_sem.at[2], recv_sem=ghost_sem,
        device_id={"panel": 1 - p}, device_id_type=MESH)
    ghost_copy.start()

    loads[1].wait()
    loads[2].wait()
    for k in range(TILES):
        words[k] = pack_vel(vt[:, 128 * k : 128 * (k + 1)], vp[:, 128 * k : 128 * (k + 1)])

    def vel_group(q, carry):
        rows = []
        for t in ORDER:
            parts = [words[q * 3 + k, pl.ds(t, LEV, stride=ROWS), :] for k in range(3)]
            rows.append(jnp.concatenate(parts, axis=1))
        for d, row in enumerate(swap_chunks(rows)):
            vel_out[q * 8 + d] = row
        return carry

    lax.fori_loop(0, GROUPS, vel_group, 0)

    def scatter(src, dst, lanes, send, recv):
        def part(ref, i):
            return ref.at[i] if lanes is None else ref.at[i, :, lanes]

        def one(s, carry):
            d = lax.rem(me + s, COLS)
            pltpu.make_async_remote_copy(
                src_ref=part(src, d), dst_ref=part(dst, me), send_sem=send, recv_sem=recv,
                device_id={"col": d}, device_id_type=MESH).start()
            return carry

        lax.fori_loop(1, COLS, one, 0)
        pltpu.make_async_copy(part(src, me), part(dst, me), recv).start()

    def scatter_group(src, dst, q, send, recv):
        for j in range(8):
            d = q * 8 + j

            @pl.when(d != me)
            def _():
                pltpu.make_async_remote_copy(
                    src_ref=src.at[d], dst_ref=dst.at[me], send_sem=send, recv_sem=recv,
                    device_id={"col": d}, device_id_type=MESH).start()

            @pl.when(d == me)
            def _():
                pltpu.make_async_copy(src.at[d], dst.at[d], recv).start()

    own_group = lax.div(me, 8)

    def arrived(dst, lanes, recv):
        whole = dst if lanes is None else dst.at[:, :, lanes]
        pltpu.make_async_copy(whole, whole, recv).wait()

    def sent(src, lanes, send):
        most = src.at[pl.ds(0, COLS - 1)] if lanes is None else src.at[pl.ds(0, COLS - 1), :, lanes]
        pltpu.make_async_copy(most, most, send).wait()

    first_part, second_part, third_part = (pl.ds(128 * i, 128) for i in range(3))
    scatter(vel_out, vel_in, first_part, send_sem.at[3], vela_sem)

    ghost_copy.wait_recv()

    wide = lax.broadcasted_iota(I32, (LEV, NPH), 1)
    ghosts = ghost_in[...]

    def star_row(place):
        t = ORDER[place]
        center = state[t]
        south = state[t - 1] if t > 0 else halo[0]
        north = state[t + 1] if t < ROWS - 1 else halo[1]
        west = jnp.where(wide == 0, ghosts[:, 2 * t : 2 * t + 1], pltpu.roll(center, 1, 1))
        east = jnp.where(wide == NPH - 1, ghosts[:, 2 * t + 1 : 2 * t + 2], pltpu.roll(center, NPH - 1, 1))
        word = jnp.concatenate(
            [words[k, pl.ds(t, LEV, stride=ROWS), :] for k in range(TILES)], axis=1)
        half_t, half_p = half_vel(word)
        star[place] = (
            center + KAPPA * (north + south + east + west - 4.0 * center)
            - half_t * (north - south) - half_p * (east - west)
        )

    for place in range(6):
        star_row(place)

    def early_group(i, carry):
        q = lax.rem(own_group + i, GROUPS)
        lanes = pl.ds(pl.multiple_of(q * CELLS, 128), CELLS)
        rows = swap_chunks([star[place if place < 6 else 0, :, lanes] for place in range(ROWS)])
        for d, row in enumerate(rows):
            word, k = encode_early(row[:, 0:128], row[:, 128:256])
            early_out[q * 8 + d] = word
            scales[pl.ds(pl.multiple_of(q * 64 + 8 * d, 8), 8), :] = k
        scatter_group(early_out, early_in, q, send_sem.at[4], early_sem)
        return carry

    lax.fori_loop(0, GROUPS, early_group, 0)

    def unpack_row(i):
        for q in range(GROUPS):
            parts = decode(row_in[i, :, 256 * q : 256 * q + 128], row_in[i, :, 256 * q + 128 : 256 * (q + 1)])
            for k, part in enumerate(parts):
                halo[i, :, CELLS * q + 128 * k : CELLS * q + 128 * (k + 1)] = part

    @pl.when(g > 0)
    def _():
        up.wait_recv()
        unpack_row(0)

    @pl.when(g < 7)
    def _():
        down.wait_recv()
        unpack_row(1)

    star_row(6)
    star_row(7)

    def late_group(i, carry):
        q = lax.rem(own_group + i, GROUPS)
        lanes = pl.ds(pl.multiple_of(q * CELLS, 128), CELLS)
        rows = swap_chunks([star[place, :, lanes] for place in range(ROWS)])
        for d, row in enumerate(rows):
            k = scales[pl.ds(pl.multiple_of(q * 64 + 8 * d, 8), 8), :]
            late_out[q * 8 + d] = encode_late(row[:, 256:384], k)
        scatter_group(late_out, late_in, q, send_sem.at[11], late_sem)
        return carry

    lax.fori_loop(0, GROUPS, late_group, 0)
    loads[3].wait()
    matrix = mat[...]
    mat_h[...], mat_l[...] = halves(matrix)
    tmat_h[...], tmat_l[...] = halves(jnp.transpose(matrix))

    sent(early_out, None, send_sem.at[4])
    sent(late_out, None, send_sem.at[11])
    scatter(vel_out, vel_in, second_part, send_sem.at[5], velb_sem)
    arrived(early_in, None, early_sem)
    arrived(late_in, None, late_sem)
    scatter(vel_out, vel_in, third_part, send_sem.at[13], velc_sem)
    tiles1 = decode_tiles(early_in[...].reshape(NR, 128), late_in[...].reshape(NR, 128))
    for i, tile in enumerate(tiles1):
        star_col[pl.ds(128 * i, 128), :] = jnp.transpose(tile)
    first = dot3(halves(star_col[...]), (tmat_h[...], tmat_l[...]), ((1,), (0,)))
    for place, t in enumerate(ORDER):
        column[t, pl.ds(8, PHD), :] = first[place * PHD : (place + 1) * PHD]

    @pl.when(g == 0)
    def _():
        side[0] = jnp.zeros((PHD, NR), F32)

    @pl.when(g == 7)
    def _():
        side[1] = jnp.zeros((PHD, NR), F32)

    inner = pl.ds(8, PHD)
    for i, t in enumerate((ROWS - 1, 0)):
        w0, w1 = encode(*(column[t, 8 + 16 * k : 24 + 16 * k, :] for k in range(3)), axis=0)
        side_out[i, 0:16, :] = w0
        side_out[i, 16:32, :] = w1

    def side_copy(sem, target):
        return pltpu.make_async_remote_copy(
            src_ref=side_out.at[sem], dst_ref=side_in.at[sem], send_sem=send_sem.at[sem + 6],
            recv_sem=side_sem.at[sem], device_id={"grp": target}, device_id_type=MESH)

    up2 = side_copy(0, g + 1)
    down2 = side_copy(1, g - 1)

    @pl.when(g < 7)
    def _():
        up2.start()

    @pl.when(g > 0)
    def _():
        down2.start()

    for s in range(2):
        at_end = me == s * (COLS - 1)
        for t in range(ROWS):
            cell = cell_ref[s, t]
            d = dir_ref[s, t]
            r = lax.div(cell, NPH)
            c = jnp.clip(cell - r * NPH - s * (NPH - PHD), 0, PHD - 2)
            own = s * (PHD - 1)
            row1 = jnp.where(at_end, r, t)
            row2 = jnp.where(at_end, r + d, t)
            col1 = jnp.where(at_end, c, own)
            col2 = jnp.where(at_end, c + 1 - d, own)
            edge_out[s, pl.ds(t, 1), :] = 0.5 * (
                column[row1, pl.ds(col1 + 8, 1), :] + column[row2, pl.ds(col2 + 8, 1), :])
    edge_copies = []
    for s in range(2):
        at_end = me == s * (COLS - 1)
        there = jnp.where(at_end, me, me + 2 * s - 1)
        panel = jnp.where(at_end, 1 - p, p)
        slot = jnp.where(at_end, s, 1 - s)
        copy = pltpu.make_async_remote_copy(
            src_ref=edge_out.at[s], dst_ref=edge_in.at[slot], send_sem=send_sem.at[8 + s], recv_sem=edge_sem.at[slot],
            device_id={"panel": panel, "col": there}, device_id_type=MESH)
        copy.start()
        edge_copies.append(copy)

    def unpack_side(i):
        for k, part in enumerate(decode(side_in[i, 0:16, :], side_in[i, 16:32, :])):
            side[i, 16 * k : 16 * (k + 1), :] = part

    def turn(i):
        vel_col[pl.ds(128 * i, 128), :] = jnp.transpose(vel_in[:, :, 128 * i : 128 * (i + 1)].reshape(NR, 128))

    arrived(vel_in, first_part, vela_sem)
    arrived(vel_in, second_part, velb_sem)
    turn(0)
    turn(1)

    for s in range(2):
        pltpu.make_async_copy(edge_in.at[s], edge_in.at[s], edge_sem.at[s]).wait()
    for t in range(ROWS):
        column[t, pl.ds(7, 1), :] = edge_in[0, pl.ds(t, 1), :]
        column[t, pl.ds(8 + PHD, 1), :] = edge_in[1, pl.ds(t, 1), :]

    def column_star(place, start=0, size=PHD):
        t = ORDER[place]
        part = pl.ds(8 + start, size)
        center = column[t, part, :]
        south = column[t - 1, part, :] if t > 0 else side[0]
        north = column[t + 1, part, :] if t < ROWS - 1 else side[1]
        east = column[t, pl.ds(9 + start, size), :]
        west = column[t, pl.ds(7 + start, size), :]
        half_t, half_p = half_vel(vel_col[pl.ds(place * PHD + start, size), :])
        star_col[pl.ds(place * PHD + start, size), :] = (
            center + KAPPA * (north + south + east + west - 4.0 * center)
            - half_t * (north - south) - half_p * (east - west)
        )

    matrix_halves = mat_h[...], mat_l[...]
    for place in range(5):
        column_star(place)
    column_star(5, 0, 16)
    solved[:, 0:256] = dot3(matrix_halves, halves(star_col[0:256]), ((1,), (1,)))

    arrived(vel_in, third_part, velc_sem)
    turn(2)
    column_star(5, 16, 32)

    @pl.when(g > 0)
    def _():
        up2.wait_recv()
        unpack_side(0)

    @pl.when(g < 7)
    def _():
        down2.wait_recv()
        unpack_side(1)

    column_star(6)
    column_star(7)
    solved[:, 256:384] = dot3(matrix_halves, halves(star_col[256:384]), ((1,), (1,)))

    def back_group(i, carry):
        q = lax.rem(own_group + i, GROUPS)
        rows = pl.ds(pl.multiple_of(q * 64, 64), 64)
        word, k = encode_early(solved[rows, 0:128], solved[rows, 128:256])
        late = encode_late(solved[rows, 256:384], k)
        back_out[pl.ds(q * 8, 8), :, 0:128] = word.reshape(8, LEV, 128)
        back_out[pl.ds(q * 8, 8), :, 128:256] = late.reshape(8, LEV, 128)
        scatter_group(back_out, back_in, q, send_sem.at[10], back_sem.at[own_group])
        return carry

    lax.fori_loop(0, GROUPS, back_group, 0)

    @pl.when(g < 7)
    def _():
        up.wait_send()
        up2.wait_send()

    @pl.when(g > 0)
    def _():
        down.wait_send()
        down2.wait_send()

    ghost_copy.wait_send()
    for copy in edge_copies:
        copy.wait_send()
    sent(vel_out, first_part, send_sem.at[3])
    sent(vel_out, second_part, send_sem.at[5])
    sent(vel_out, third_part, send_sem.at[13])

    def out_group(i, carry):
        q = lax.rem(own_group + GROUPS - i, GROUPS)
        part = back_in.at[pl.ds(q * 8, 8)]
        pltpu.make_async_copy(part, part, back_sem.at[q]).wait()
        rows = []
        for d in range(8):
            rows.append(jnp.concatenate(decode_tiles(back_in[q * 8 + d, :, 0:128], back_in[q * 8 + d, :, 128:256]), axis=1))
        for t, row in zip(ORDER, swap_chunks(rows)):
            for k in range(3):
                tiles[q * 3 + k, pl.ds(t, LEV, stride=ROWS), :] = row[:, 128 * k : 128 * (k + 1)]
        for k in range(3):
            lanes = pl.ds(pl.multiple_of(q * CELLS + 128 * k, 128), 128)
            pltpu.make_async_copy(tiles.at[q * 3 + k], out_ref.at[:, lanes], load_sem.at[4]).start()
        return carry

    lax.fori_loop(0, GROUPS, out_group, 0)
    pltpu.make_async_copy(tiles, tiles, load_sem.at[4]).wait()
    sent(back_out, None, send_sem.at[10])


def per_device(field, vel_theta, vel_phi, strip_cell, strip_dir, radial_inverse):
    smem = pl.BlockSpec(memory_space=pltpu.SMEM)
    hbm = pl.BlockSpec(memory_space=pl.ANY)
    flat = (LEV * ROWS, NPH)
    tiled = (TILES, LEV * ROWS, 128)
    dma = pltpu.SemaphoreType.DMA
    out = pl.pallas_call(
        kernel,
        out_shape=jax.ShapeDtypeStruct(flat, F32),
        in_specs=[smem, smem, hbm, hbm, hbm, hbm],
        out_specs=pl.BlockSpec(memory_space=pl.ANY),
        scratch_shapes=[
            pltpu.VMEM(tiled, F32), pltpu.VMEM(flat, BF16), pltpu.VMEM(flat, BF16), pltpu.VMEM((NR, NR), F32),
            pltpu.VMEM((NR, NR), BF16), pltpu.VMEM((NR, NR), BF16), pltpu.VMEM((NR, NR), BF16), pltpu.VMEM((NR, NR), BF16),
            pltpu.VMEM((ROWS, LEV, NPH), F32), pltpu.VMEM((2, LEV, 1024), I32), pltpu.VMEM((2, LEV, 1024), I32), pltpu.VMEM((2, LEV, NPH), F32), pltpu.VMEM(tiled, I32), pltpu.VMEM((ROWS, LEV, NPH), F32),
            pltpu.VMEM((LEV, 128), F32), pltpu.VMEM((LEV, 128), F32),
            pltpu.VMEM((COLS, LEV, CELLS), I32), pltpu.VMEM((COLS, LEV, CELLS), I32),
            *[pltpu.VMEM((COLS, LEV, 128), I32)] * 4, *[pltpu.VMEM((COLS, LEV, 256), I32)] * 2, pltpu.VMEM((NR, 128), I32),
            pltpu.VMEM((ROWS, 64, NR), F32), pltpu.VMEM((2, 32, NR), I32), pltpu.VMEM((2, 32, NR), I32), pltpu.VMEM((2, PHD, NR), F32),
            pltpu.VMEM((2, ROWS, NR), F32), pltpu.VMEM((2, ROWS, NR), F32),
            pltpu.VMEM((CELLS, NR), I32), pltpu.VMEM((CELLS, NR), F32), pltpu.VMEM((NR, CELLS), F32), pltpu.VMEM(tiled, F32),
            dma((5,)), dma((14,)), dma((2,)), dma, dma, dma, dma, dma, dma,
            dma((GROUPS,)), dma((2,)), dma((2,)),
        ],
        compiler_params=pltpu.CompilerParams(
            collective_id=0, has_side_effects=True, vmem_limit_bytes=60 * 2**20),
    )(
        strip_cell[0].T, strip_dir[0].T, field.reshape(flat), vel_theta.reshape(flat), vel_phi.reshape(flat),
        radial_inverse,
    )
    return out.reshape(1, LEV, ROWS, NPH)


def solution(mesh):
    placed = (
        P("panel", "col", "grp", None),
        P("panel", "col", "grp", None),
        P("panel", "col", "grp", None),
        P("panel", "grp", None),
        P("panel", "grp", None),
        P(),
    )
    return jax.shard_map(
        per_device, mesh=mesh, in_specs=placed, out_specs=P("panel", "col", "grp", None), check_vma=False)
```

```python
import functools

import jax
import jax.numpy as jnp
from jax import lax
from jax.experimental import pallas as pl
from jax.experimental.pallas import tpu as pltpu
from jax.sharding import PartitionSpec as P

MESH = pl.DeviceIdType.MESH
KAPPA = 0.2
COLS = 32
LEV = 8
ROWS = 8
NPH = 1536
PHD = 48
NR = 256
CELLS = ROWS * PHD
GROUPS = NPH // CELLS
TILES = NPH // 128
VEL_ONE = 32767.0
ORDER = (1, 2, 3, 4, 5, 6, 0, 7)
F32 = jnp.float32
I32 = jnp.int32
BF16 = jnp.bfloat16


def to_int(x):
    return (x + jnp.where(x >= 0.0, 0.5, -0.5)).astype(I32)


def pack_vel(vt, vp):
    qt = to_int(vt.astype(F32) * VEL_ONE)
    qp = to_int(vp.astype(F32) * VEL_ONE)
    return (qt & 0xFFFF) | (qp << 16)


def half_vel(word):
    scale = 0.5 / VEL_ONE
    return ((word << 16) >> 16).astype(F32) * scale, (word >> 16).astype(F32) * scale


def swap_chunks(rows):
    lane = lax.broadcasted_iota(I32, rows[0].shape, 1)
    chunk = (lane * 1366) >> 16
    rows = list(rows)
    for bit in (1, 2, 4):
        inside = (chunk & bit) != 0
        for low in range(8):
            if low & bit:
                continue
            a, b = rows[low], rows[low | bit]
            rows[low] = jnp.where(inside, pltpu.roll(b, PHD * bit, 1), a)
            rows[low | bit] = jnp.where(inside, b, pltpu.roll(a, CELLS - PHD * bit, 1))
    return rows


def encode(x0, x1, x2, axis=1):
    top = jnp.maximum(jnp.maximum(jnp.abs(x0), jnp.abs(x1)), jnp.abs(x2))
    top = jnp.max(top, axis=axis, keepdims=True)
    top = jnp.broadcast_to(jnp.maximum(top, 1e-30), x0.shape)
    k = jnp.ceil(jnp.log2(top) * 4.0).astype(I32) + (1 - 4 * 17)
    inverse = jnp.exp2(k.astype(F32) * -0.25)
    q0, q1, q2 = (to_int(x * inverse) for x in (x0, x1, x2))
    return (
        (q0 << 14) | ((q1 >> 4) & 0x3FFF),
        (q2 << 14) | ((q1 & 15) << 10) | (k & 0x3FF),
    )


def decode(w0, w1):
    scale = jnp.exp2(((w1 << 22) >> 22).astype(F32) * 0.25)
    q1 = (((w0 << 18) >> 18) << 4) | ((w1 >> 10) & 15)
    return (
        (w0 >> 14).astype(F32) * scale,
        q1.astype(F32) * scale,
        (w1 >> 14).astype(F32) * scale,
    )


def scale_code(top, bits):
    top = jnp.maximum(jnp.max(top, axis=1, keepdims=True), 1e-30)
    return jnp.ceil(jnp.log2(jnp.broadcast_to(top, (top.shape[0], 128))) * 4.0).astype(I32) + (1 - 4 * bits)


def quarter_power(k):
    return jnp.exp2(k.astype(F32) * 0.25)


def encode_early(x0, x1):
    k = scale_code(jnp.maximum(jnp.abs(x0), jnp.abs(x1)), 15)
    inverse = quarter_power(-k)
    return (to_int(x0 * inverse) & 0xFFFF) | (to_int(x1 * inverse) << 16), k


def encode_late(x, early):
    k = scale_code(jnp.abs(x), 19)
    lane = lax.broadcasted_iota(I32, x.shape, 1)
    return (to_int(x * quarter_power(-k)) << 12) | (jnp.where(lane < 64, early, k) & 0xFFF)


def decode_tiles(early, late):
    k = (late << 20) >> 20
    scale_early = jnp.broadcast_to(quarter_power(k[:, 0:1]), late.shape)
    scale_late = jnp.broadcast_to(quarter_power(k[:, 127:128]), late.shape)
    return (
        ((early << 16) >> 16).astype(F32) * scale_early,
        (early >> 16).astype(F32) * scale_early,
        (late >> 12).astype(F32) * scale_late,
    )


def halves(x):
    high = x.astype(BF16)
    return high, (x - high.astype(F32)).astype(BF16)


def dot3(a, b, dims):
    ah, al = a
    bh, bl = b
    mul = functools.partial(lax.dot_general, dimension_numbers=(dims, ((), ())), preferred_element_type=F32)
    return mul(ah, bh) + (mul(ah, bl) + mul(al, bh))


def kernel(
    cell_ref, dir_ref, field_hbm, vt_hbm, vp_hbm, mat_hbm,
    out_ref,
    field, vt, vp, mat, mat_h, mat_l, tmat_h, tmat_l,
    state, row_out, row_in, halo, words, star, ghost_out, ghost_in,
    vel_out, vel_in, early_out, early_in, late_out, late_in,
    back_out, back_in, scales,
    column, side_out, side_in, side, edge_out, edge_in, vel_col, star_col, solved, tiles,
    load_sem, send_sem, row_sem, ghost_sem, vela_sem, velb_sem, velc_sem, early_sem, late_sem,
    back_sem, side_sem, edge_sem,
):
    p = lax.axis_index("panel")
    g = lax.axis_index("grp")
    me = lax.axis_index("col")

    for k in range(TILES):
        pltpu.make_async_copy(field_hbm.at[:, pl.ds(128 * k, 128)], field.at[k], load_sem.at[0]).start()
    loads = [
        pltpu.make_async_copy(src, dst, load_sem.at[i])
        for i, (src, dst) in enumerate(((field, field), (vt_hbm, vt), (vp_hbm, vp), (mat_hbm, mat)))
    ]
    for copy in loads[1:]:
        copy.start()

    barrier = pltpu.get_barrier_semaphore()

    def greet(s, carry):
        pl.semaphore_signal(barrier, inc=1, device_id={"col": lax.rem(me + s, COLS)}, device_id_type=MESH)
        return carry

    lax.fori_loop(1, COLS, greet, 0)
    pl.semaphore_signal(barrier, inc=1, device_id={"panel": 1 - p}, device_id_type=MESH)

    @pl.when(g > 0)
    def _():
        pl.semaphore_signal(barrier, inc=1, device_id={"grp": g - 1}, device_id_type=MESH)

    @pl.when(g < 7)
    def _():
        pl.semaphore_signal(barrier, inc=1, device_id={"grp": g + 1}, device_id_type=MESH)

    loads[0].wait()
    for t in range(ROWS):
        for k in range(TILES):
            lanes = pl.ds(128 * k, 128)
            state[t, :, lanes] = field[k, pl.ds(t, LEV, stride=ROWS), :]

    @pl.when(g == 0)
    def _():
        halo[0] = jnp.zeros((LEV, NPH), F32)

    @pl.when(g == 7)
    def _():
        halo[1] = jnp.zeros((LEV, NPH), F32)

    for i, t in enumerate((ROWS - 1, 0)):
        for q in range(GROUPS):
            w0, w1 = encode(*(state[t, :, CELLS * q + 128 * k : CELLS * q + 128 * (k + 1)] for k in range(3)))
            row_out[i, :, 256 * q : 256 * q + 128] = w0
            row_out[i, :, 256 * q + 128 : 256 * (q + 1)] = w1

    count = COLS + jnp.where(g > 0, 1, 0) + jnp.where(g < 7, 1, 0)
    pl.semaphore_wait(barrier, count)

    def row_copy(sem, target):
        return pltpu.make_async_remote_copy(
            src_ref=row_out.at[sem], dst_ref=row_in.at[sem], send_sem=send_sem.at[sem], recv_sem=row_sem.at[sem],
            device_id={"grp": target}, device_id_type=MESH)

    up = row_copy(0, g + 1)
    down = row_copy(1, g - 1)

    @pl.when(g < 7)
    def _():
        up.start()

    @pl.when(g > 0)
    def _():
        down.start()

    lane = lax.broadcasted_iota(I32, (LEV, 128), 1)
    ghosts = jnp.zeros((LEV, 128), F32)
    for t in range(ROWS):
        for s in range(2):
            cell = cell_ref[s, t]
            d = dir_ref[s, t]
            r = lax.div(cell, NPH)
            c = cell - r * NPH - s * (NPH - 128)
            lanes = pl.ds(s * (NPH - 128), 128)
            first = state[r, :, lanes]
            second = state[r + d, :, lanes]
            both = jnp.where(lane == c, first, 0.0) + jnp.where(lane == c + 1 - d, second, 0.0)
            value = 0.5 * jnp.sum(both, axis=1, keepdims=True)
            ghosts = jnp.where(lane == 2 * t + s, value, ghosts)
    ghost_out[...] = ghosts

    ghost_copy = pltpu.make_async_remote_copy(
        src_ref=ghost_out, dst_ref=ghost_in, send_sem=send_sem.at[2], recv_sem=ghost_sem,
        device_id={"panel": 1 - p}, device_id_type=MESH)
    ghost_copy.start()

    loads[1].wait()
    loads[2].wait()
    for k in range(TILES):
        words[k] = pack_vel(vt[:, 128 * k : 128 * (k + 1)], vp[:, 128 * k : 128 * (k + 1)])

    def vel_group(q, carry):
        rows = []
        for t in ORDER:
            parts = [words[q * 3 + k, pl.ds(t, LEV, stride=ROWS), :] for k in range(3)]
            rows.append(jnp.concatenate(parts, axis=1))
        for d, row in enumerate(swap_chunks(rows)):
            vel_out[q * 8 + d] = row
        return carry

    lax.fori_loop(0, GROUPS, vel_group, 0)

    def scatter(src, dst, lanes, send, recv):
        def part(ref, i):
            return ref.at[i] if lanes is None else ref.at[i, :, lanes]

        def one(s, carry):
            d = lax.rem(me + s, COLS)
            pltpu.make_async_remote_copy(
                src_ref=part(src, d), dst_ref=part(dst, me), send_sem=send, recv_sem=recv,
                device_id={"col": d}, device_id_type=MESH).start()
            return carry

        lax.fori_loop(1, COLS, one, 0)
        pltpu.make_async_copy(part(src, me), part(dst, me), recv).start()

    def scatter_group(src, dst, q, send, recv):
        for j in range(8):
            d = q * 8 + j

            @pl.when(d != me)
            def _():
                pltpu.make_async_remote_copy(
                    src_ref=src.at[d], dst_ref=dst.at[me], send_sem=send, recv_sem=recv,
                    device_id={"col": d}, device_id_type=MESH).start()

            @pl.when(d == me)
            def _():
                pltpu.make_async_copy(src.at[d], dst.at[d], recv).start()

    own_group = lax.div(me, 8)

    def arrived(dst, lanes, recv):
        whole = dst if lanes is None else dst.at[:, :, lanes]
        pltpu.make_async_copy(whole, whole, recv).wait()

    def sent(src, lanes, send):
        most = src.at[pl.ds(0, COLS - 1)] if lanes is None else src.at[pl.ds(0, COLS - 1), :, lanes]
        pltpu.make_async_copy(most, most, send).wait()

    first_part, second_part, third_part = (pl.ds(128 * i, 128) for i in range(3))
    scatter(vel_out, vel_in, first_part, send_sem.at[3], vela_sem)

    ghost_copy.wait_recv()

    wide = lax.broadcasted_iota(I32, (LEV, NPH), 1)
    ghosts = ghost_in[...]

    def star_row(place):
        t = ORDER[place]
        center = state[t]
        south = state[t - 1] if t > 0 else halo[0]
        north = state[t + 1] if t < ROWS - 1 else halo[1]
        west = jnp.where(wide == 0, ghosts[:, 2 * t : 2 * t + 1], pltpu.roll(center, 1, 1))
        east = jnp.where(wide == NPH - 1, ghosts[:, 2 * t + 1 : 2 * t + 2], pltpu.roll(center, NPH - 1, 1))
        word = jnp.concatenate(
            [words[k, pl.ds(t, LEV, stride=ROWS), :] for k in range(TILES)], axis=1)
        half_t, half_p = half_vel(word)
        star[place] = (
            center + KAPPA * (north + south + east + west - 4.0 * center)
            - half_t * (north - south) - half_p * (east - west)
        )

    for place in range(6):
        star_row(place)

    def early_group(i, carry):
        q = lax.rem(own_group + i, GROUPS)
        lanes = pl.ds(pl.multiple_of(q * CELLS, 128), CELLS)
        rows = swap_chunks([star[place if place < 6 else 0, :, lanes] for place in range(ROWS)])
        for d, row in enumerate(rows):
            word, k = encode_early(row[:, 0:128], row[:, 128:256])
            early_out[q * 8 + d] = word
            scales[pl.ds(pl.multiple_of(q * 64 + 8 * d, 8), 8), :] = k
        scatter_group(early_out, early_in, q, send_sem.at[4], early_sem)
        return carry

    lax.fori_loop(0, GROUPS, early_group, 0)

    def unpack_row(i):
        for q in range(GROUPS):
            parts = decode(row_in[i, :, 256 * q : 256 * q + 128], row_in[i, :, 256 * q + 128 : 256 * (q + 1)])
            for k, part in enumerate(parts):
                halo[i, :, CELLS * q + 128 * k : CELLS * q + 128 * (k + 1)] = part

    @pl.when(g > 0)
    def _():
        up.wait_recv()
        unpack_row(0)

    @pl.when(g < 7)
    def _():
        down.wait_recv()
        unpack_row(1)

    star_row(6)
    star_row(7)

    def late_group(i, carry):
        q = lax.rem(own_group + i, GROUPS)
        lanes = pl.ds(pl.multiple_of(q * CELLS, 128), CELLS)
        rows = swap_chunks([star[place, :, lanes] for place in range(ROWS)])
        for d, row in enumerate(rows):
            k = scales[pl.ds(pl.multiple_of(q * 64 + 8 * d, 8), 8), :]
            late_out[q * 8 + d] = encode_late(row[:, 256:384], k)
        scatter_group(late_out, late_in, q, send_sem.at[11], late_sem)
        return carry

    lax.fori_loop(0, GROUPS, late_group, 0)
    loads[3].wait()
    matrix = mat[...]
    mat_h[...], mat_l[...] = halves(matrix)
    tmat_h[...], tmat_l[...] = halves(jnp.transpose(matrix))

    sent(early_out, None, send_sem.at[4])
    sent(late_out, None, send_sem.at[11])
    scatter(vel_out, vel_in, second_part, send_sem.at[5], velb_sem)
    arrived(early_in, None, early_sem)
    arrived(late_in, None, late_sem)
    tiles1 = decode_tiles(early_in[...].reshape(NR, 128), late_in[...].reshape(NR, 128))
    for i, tile in enumerate(tiles1):
        star_col[pl.ds(128 * i, 128), :] = jnp.transpose(tile)
    first = dot3(halves(star_col[...]), (tmat_h[...], tmat_l[...]), ((1,), (0,)))
    for place, t in enumerate(ORDER):
        column[t, pl.ds(8, PHD), :] = first[place * PHD : (place + 1) * PHD]

    @pl.when(g == 0)
    def _():
        side[0] = jnp.zeros((PHD, NR), F32)

    @pl.when(g == 7)
    def _():
        side[1] = jnp.zeros((PHD, NR), F32)

    inner = pl.ds(8, PHD)
    for i, t in enumerate((ROWS - 1, 0)):
        w0, w1 = encode(*(column[t, 8 + 16 * k : 24 + 16 * k, :] for k in range(3)), axis=0)
        side_out[i, 0:16, :] = w0
        side_out[i, 16:32, :] = w1

    def side_copy(sem, target):
        return pltpu.make_async_remote_copy(
            src_ref=side_out.at[sem], dst_ref=side_in.at[sem], send_sem=send_sem.at[sem + 6],
            recv_sem=side_sem.at[sem], device_id={"grp": target}, device_id_type=MESH)

    up2 = side_copy(0, g + 1)
    down2 = side_copy(1, g - 1)

    @pl.when(g < 7)
    def _():
        up2.start()

    @pl.when(g > 0)
    def _():
        down2.start()

    for s in range(2):
        at_end = me == s * (COLS - 1)
        for t in range(ROWS):
            cell = cell_ref[s, t]
            d = dir_ref[s, t]
            r = lax.div(cell, NPH)
            c = jnp.clip(cell - r * NPH - s * (NPH - PHD), 0, PHD - 2)
            own = s * (PHD - 1)
            row1 = jnp.where(at_end, r, t)
            row2 = jnp.where(at_end, r + d, t)
            col1 = jnp.where(at_end, c, own)
            col2 = jnp.where(at_end, c + 1 - d, own)
            edge_out[s, pl.ds(t, 1), :] = 0.5 * (
                column[row1, pl.ds(col1 + 8, 1), :] + column[row2, pl.ds(col2 + 8, 1), :])
    edge_copies = []
    for s in range(2):
        at_end = me == s * (COLS - 1)
        there = jnp.where(at_end, me, me + 2 * s - 1)
        panel = jnp.where(at_end, 1 - p, p)
        slot = jnp.where(at_end, s, 1 - s)
        copy = pltpu.make_async_remote_copy(
            src_ref=edge_out.at[s], dst_ref=edge_in.at[slot], send_sem=send_sem.at[8 + s], recv_sem=edge_sem.at[slot],
            device_id={"panel": panel, "col": there}, device_id_type=MESH)
        copy.start()
        edge_copies.append(copy)

    scatter(vel_out, vel_in, third_part, send_sem.at[13], velc_sem)

    def unpack_side(i):
        for k, part in enumerate(decode(side_in[i, 0:16, :], side_in[i, 16:32, :])):
            side[i, 16 * k : 16 * (k + 1), :] = part

    def turn(i):
        vel_col[pl.ds(128 * i, 128), :] = jnp.transpose(vel_in[:, :, 128 * i : 128 * (i + 1)].reshape(NR, 128))

    arrived(vel_in, first_part, vela_sem)
    arrived(vel_in, second_part, velb_sem)
    turn(0)
    turn(1)

    for s in range(2):
        pltpu.make_async_copy(edge_in.at[s], edge_in.at[s], edge_sem.at[s]).wait()
    for t in range(ROWS):
        column[t, pl.ds(7, 1), :] = edge_in[0, pl.ds(t, 1), :]
        column[t, pl.ds(8 + PHD, 1), :] = edge_in[1, pl.ds(t, 1), :]

    def column_star(place, start=0, size=PHD):
        t = ORDER[place]
        part = pl.ds(8 + start, size)
        center = column[t, part, :]
        south = column[t - 1, part, :] if t > 0 else side[0]
        north = column[t + 1, part, :] if t < ROWS - 1 else side[1]
        east = column[t, pl.ds(9 + start, size), :]
        west = column[t, pl.ds(7 + start, size), :]
        half_t, half_p = half_vel(vel_col[pl.ds(place * PHD + start, size), :])
        star_col[pl.ds(place * PHD + start, size), :] = (
            center + KAPPA * (north + south + east + west - 4.0 * center)
            - half_t * (north - south) - half_p * (east - west)
        )

    matrix_halves = mat_h[...], mat_l[...]
    for place in range(5):
        column_star(place)
    column_star(5, 0, 16)
    solved[:, 0:256] = dot3(matrix_halves, halves(star_col[0:256]), ((1,), (1,)))

    arrived(vel_in, third_part, velc_sem)
    turn(2)
    column_star(5, 16, 32)

    @pl.when(g > 0)
    def _():
        up2.wait_recv()
        unpack_side(0)

    @pl.when(g < 7)
    def _():
        down2.wait_recv()
        unpack_side(1)

    column_star(6)
    column_star(7)
    solved[:, 256:384] = dot3(matrix_halves, halves(star_col[256:384]), ((1,), (1,)))

    def back_group(i, carry):
        q = lax.rem(own_group + i, GROUPS)
        rows = pl.ds(pl.multiple_of(q * 64, 64), 64)
        word, k = encode_early(solved[rows, 0:128], solved[rows, 128:256])
        late = encode_late(solved[rows, 256:384], k)
        back_out[pl.ds(q * 8, 8), :, 0:128] = word.reshape(8, LEV, 128)
        back_out[pl.ds(q * 8, 8), :, 128:256] = late.reshape(8, LEV, 128)
        scatter_group(back_out, back_in, q, send_sem.at[10], back_sem.at[own_group])
        return carry

    lax.fori_loop(0, GROUPS, back_group, 0)

    @pl.when(g < 7)
    def _():
        up.wait_send()
        up2.wait_send()

    @pl.when(g > 0)
    def _():
        down.wait_send()
        down2.wait_send()

    ghost_copy.wait_send()
    for copy in edge_copies:
        copy.wait_send()
    sent(vel_out, first_part, send_sem.at[3])
    sent(vel_out, second_part, send_sem.at[5])
    sent(vel_out, third_part, send_sem.at[13])

    def out_group(i, carry):
        q = lax.rem(own_group + GROUPS - i, GROUPS)
        part = back_in.at[pl.ds(q * 8, 8)]
        pltpu.make_async_copy(part, part, back_sem.at[q]).wait()
        rows = []
        for d in range(8):
            rows.append(jnp.concatenate(decode_tiles(back_in[q * 8 + d, :, 0:128], back_in[q * 8 + d, :, 128:256]), axis=1))
        for t, row in zip(ORDER, swap_chunks(rows)):
            for k in range(3):
                tiles[q * 3 + k, pl.ds(t, LEV, stride=ROWS), :] = row[:, 128 * k : 128 * (k + 1)]
        for k in range(3):
            lanes = pl.ds(pl.multiple_of(q * CELLS + 128 * k, 128), 128)
            pltpu.make_async_copy(tiles.at[q * 3 + k], out_ref.at[:, lanes], load_sem.at[4]).start()
        return carry

    lax.fori_loop(0, GROUPS, out_group, 0)
    pltpu.make_async_copy(tiles, tiles, load_sem.at[4]).wait()
    sent(back_out, None, send_sem.at[10])


def per_device(field, vel_theta, vel_phi, strip_cell, strip_dir, radial_inverse):
    smem = pl.BlockSpec(memory_space=pltpu.SMEM)
    hbm = pl.BlockSpec(memory_space=pl.ANY)
    flat = (LEV * ROWS, NPH)
    tiled = (TILES, LEV * ROWS, 128)
    dma = pltpu.SemaphoreType.DMA
    out = pl.pallas_call(
        kernel,
        out_shape=jax.ShapeDtypeStruct(flat, F32),
        in_specs=[smem, smem, hbm, hbm, hbm, hbm],
        out_specs=pl.BlockSpec(memory_space=pl.ANY),
        scratch_shapes=[
            pltpu.VMEM(tiled, F32), pltpu.VMEM(flat, BF16), pltpu.VMEM(flat, BF16), pltpu.VMEM((NR, NR), F32),
            pltpu.VMEM((NR, NR), BF16), pltpu.VMEM((NR, NR), BF16), pltpu.VMEM((NR, NR), BF16), pltpu.VMEM((NR, NR), BF16),
            pltpu.VMEM((ROWS, LEV, NPH), F32), pltpu.VMEM((2, LEV, 1024), I32), pltpu.VMEM((2, LEV, 1024), I32), pltpu.VMEM((2, LEV, NPH), F32), pltpu.VMEM(tiled, I32), pltpu.VMEM((ROWS, LEV, NPH), F32),
            pltpu.VMEM((LEV, 128), F32), pltpu.VMEM((LEV, 128), F32),
            pltpu.VMEM((COLS, LEV, CELLS), I32), pltpu.VMEM((COLS, LEV, CELLS), I32),
            *[pltpu.VMEM((COLS, LEV, 128), I32)] * 4, *[pltpu.VMEM((COLS, LEV, 256), I32)] * 2, pltpu.VMEM((NR, 128), I32),
            pltpu.VMEM((ROWS, 64, NR), F32), pltpu.VMEM((2, 32, NR), I32), pltpu.VMEM((2, 32, NR), I32), pltpu.VMEM((2, PHD, NR), F32),
            pltpu.VMEM((2, ROWS, NR), F32), pltpu.VMEM((2, ROWS, NR), F32),
            pltpu.VMEM((CELLS, NR), I32), pltpu.VMEM((CELLS, NR), F32), pltpu.VMEM((NR, CELLS), F32), pltpu.VMEM(tiled, F32),
            dma((5,)), dma((14,)), dma((2,)), dma, dma, dma, dma, dma, dma,
            dma((GROUPS,)), dma((2,)), dma((2,)),
        ],
        compiler_params=pltpu.CompilerParams(
            collective_id=0, has_side_effects=True, vmem_limit_bytes=60 * 2**20),
    )(
        strip_cell[0].T, strip_dir[0].T, field.reshape(flat), vel_theta.reshape(flat), vel_phi.reshape(flat),
        radial_inverse,
    )
    return out.reshape(1, LEV, ROWS, NPH)


def solution(mesh):
    placed = (
        P("panel", "col", "grp", None),
        P("panel", "col", "grp", None),
        P("panel", "col", "grp", None),
        P("panel", "grp", None),
        P("panel", "grp", None),
        P(),
    )
    return jax.shard_map(
        per_device, mesh=mesh, in_specs=placed, out_specs=P("panel", "col", "grp", None), check_vma=False)
```
